256 devices in a mesh: gx: 32 (over z, y_hi, core), gy: 8 (over x, y_lo).
Axes of the slice: x: 4, y: 4 (y_hi: 2, y_lo: 2; y = y_hi * 2 + y_lo), z: 8, core: 2. Of those that a mesh axis runs over, the one named last changes fastest.
Arguments:
- cotangent: float32 [256, 64, 1024], P('gx', 'gy'), may hold values from -6 to 6
- diagonal: float32 [256, 64, 1024], P('gx', 'gy'), may hold values from 0.01 to 0.1
Outputs:
- grad_guess: float32 [256, 64, 1024], P('gx', 'gy')
- grad_source: float32 [256, 64, 1024], P('gx', 'gy')
The draws below stay inside these ranges and needn't reach their ends.
All inputs are finite; a program needn't handle non-finite values.
Results may differ from the reference program's by a relative error of at most 0.0003.
Values sent between devices are 32-bit elements; how exact they have to be, the bound alone decides.
No kernel may reach another device: no remote copies, remote signals or barrier semaphores. Data moves between devices by JAX's collectives and lax.ppermute only.
A program may use at most 128 MiB of HBM per device.

```python
import math
import jax
import jax.numpy as jnp
from jax import lax

LEVELS = 4
SMOOTHING = 2
COARSE_SWEEPS = 8
NX = 256
NY = 64
NZ = 1024


def draw_cotangent(key, part):
    key = jax.random.fold_in(key, 11)
    return jnp.clip(jax.random.normal(key, (NX, NY, NZ), jnp.float32), -6.0, 6.0)


def block_scale(stream_key, extent, cuts, least, top_value):
    gain = 1.0
    for dim, blocks in cuts:
        steps = jax.random.uniform(jax.random.fold_in(jax.random.fold_in(stream_key, 6), dim), (blocks,), jnp.float32, least / len(cuts), top_value / len(cuts))
        gain = gain * jnp.repeat(jnp.exp(steps), extent[dim] // blocks).reshape((-1,) + (1,) * (len(extent) - 1 - dim))
    return gain


def setup_inputs(seed: int = 0) -> dict:
    seeds = jax.random.split(jax.random.key(seed), 3)
    cotangent = draw_cotangent(jax.random.fold_in(seeds[2], 71), 0)
    diagonal = jnp.clip(jnp.exp(math.log(0.1) - 2.3025851 * jax.random.uniform(seeds[1], (NX, NY, NZ), jnp.float32) ** block_scale(seeds[1], (NX, NY, NZ), ((0, 32), (1, 8)), -0.2, 0.2)), 0.01, 0.1)
    return dict(cotangent=cotangent, diagonal=diagonal)


damping_weight = 2.0 / 3.0

def neighbours(field):
    total = jnp.roll(field, -1, 0) + jnp.roll(field, 1, 0)
    total = total + jnp.roll(field, -1, 1) + jnp.roll(field, 1, 1)
    return total + jnp.roll(field, 1, 2) + jnp.roll(field, -1, 2)

def operate(field, diagonal_sum):
    return diagonal_sum * field - neighbours(field)

def sweep(field, source, diagonal_sum):
    return field + damping_weight * (source - operate(field, diagonal_sum)) / diagonal_sum

def block_mean(field):
    shape_now = field.shape
    blocks = field.reshape(shape_now[0] // 2, 2, shape_now[1] // 2, 2, shape_now[2] // 2, 2)
    return lax.optimization_barrier(jnp.mean(blocks, axis=(1, 3, 5)))

def spread(field):
    return jnp.repeat(jnp.repeat(jnp.repeat(field, 2, 0), 2, 1), 2, 2)

def cycle(level_index, field, source, coefficients):
    diagonal_sum = 6.0 + 4.0 ** level_index * coefficients[level_index]
    if level_index == len(coefficients) - 1:
        field = jnp.zeros_like(source)
        for sweep_index in range(COARSE_SWEEPS):
            field = sweep(field, source, diagonal_sum)
        return field
    for sweep_index in range(SMOOTHING):
        field = sweep(field, source, diagonal_sum)
    residual = source - operate(field, diagonal_sum)
    coarse_source = 4.0 * block_mean(residual)
    correction = cycle(level_index + 1, jnp.zeros_like(coarse_source), coarse_source, coefficients)
    field = field + spread(correction)
    for sweep_index in range(SMOOTHING):
        field = sweep(field, source, diagonal_sum)
    return field

def reference(cotangent, diagonal):
    coefficients = [diagonal]
    for level_index in range(LEVELS - 1):
        coefficients.append(block_mean(coefficients[-1]))
    zero_field = jnp.zeros_like(cotangent)

    def forward(guess, source):
        return cycle(0, guess, source, coefficients)
    unused, pullback = jax.vjp(forward, zero_field, zero_field)
    grad_guess, grad_source = pullback(cotangent)
    return (grad_guess, grad_source)
```

```python
import jax
import jax.numpy as jnp
from jax import lax
from jax.experimental import pallas as pl
from jax.experimental.pallas import tpu as pltpu
from jax.sharding import PartitionSpec as P

GX = 32
GY = 8
OMEGA = 2.0 / 3.0
THIRD = 1.0 / 3.0
F32 = jnp.float32
VMEM_LIMIT = 48 * 1024 * 1024


def params():
    return pltpu.CompilerParams(vmem_limit_bytes=VMEM_LIMIT)


def shape(*dims):
    return jax.ShapeDtypeStruct(dims, F32)


def smem():
    return pl.BlockSpec(memory_space=pltpu.SMEM)


def vmem():
    return pl.BlockSpec(memory_space=pltpu.VMEM)


def z_sum_fine(v):
    last = v.ndim - 1
    place = lax.broadcasted_iota(jnp.int32, v.shape, last - 1)
    after = pltpu.roll(v, 7, last - 1)
    after = jnp.where(place == 7, pltpu.roll(after, 127, last), after)
    before = pltpu.roll(v, 1, last - 1)
    before = jnp.where(place == 0, pltpu.roll(before, 1, last), before)
    return after + before


def yz_sum(v):
    count, rows = v.shape[0], v.shape[1]
    total = pltpu.roll(v, 1, 1) + pltpu.roll(v, rows - 1, 1)
    parts = []
    for c in range(count):
        after = v[c + 1] if c < count - 1 else pltpu.roll(v[0], 127, 1)
        before = v[c - 1] if c > 0 else pltpu.roll(v[count - 1], 1, 1)
        parts.append(after + before)
    return total + jnp.stack(parts, 0)


def coarse_neighbours(ref, x):
    return ref[x + 1] + ref[x - 1] + yz_sum(ref[x])


def restrict_fine(pairs_ref, out_ref, scale):
    for x in range(4):
        for c in range(4):
            out_ref[x, c] = scale * (
                pairs_ref[x, pl.ds(2 * c, 4, stride=8), :] + pairs_ref[x, pl.ds(2 * c + 1, 4, stride=8), :]
            )


def block_pairs(field, pairs_ref):
    for x in range(4):
        row = field[2 * x] + field[2 * x + 1]
        for y in range(4):
            pairs_ref[x, pl.ds(8 * y, 8), :] = row[2 * y] + row[2 * y + 1]


def prepare_kernel(cot_ref, diag_ref, f_ref, sg_ref, ylo_ref, yhi_ref, c1_ref, turned, placed, pairs):
    stacked = jnp.concatenate([cot_ref[...].reshape(64, 1024), diag_ref[...].reshape(64, 1024)], axis=0)
    turned[...] = stacked.T
    for c in range(8):
        placed[pl.ds(c, 128, stride=8), :] = turned[pl.ds(c, 128, stride=8), :].T
    f = placed[0:512, :].reshape(8, 8, 8, 128)
    diag = placed[512:1024, :].reshape(8, 8, 8, 128)
    g = OMEGA / (6.0 + diag)
    s = g * f
    f_ref[...] = f
    sg_ref[0] = s
    sg_ref[1] = g
    ylo_ref[0] = s[:, 0:2]
    ylo_ref[1] = g[:, 0:2]
    yhi_ref[0] = s[:, 6:8]
    yhi_ref[1] = g[:, 6:8]
    block_pairs(diag, pairs)
    restrict_fine(pairs, c1_ref, 0.125)


def prepare(cot, diag):
    return pl.pallas_call(
        prepare_kernel,
        out_shape=(
            shape(8, 8, 8, 128),
            shape(2, 8, 8, 8, 128),
            shape(2, 8, 2, 8, 128),
            shape(2, 8, 2, 8, 128),
            shape(4, 4, 4, 128),
        ),
        scratch_shapes=[
            pltpu.VMEM((1024, 128), F32),
            pltpu.VMEM((1024, 128), F32),
            pltpu.VMEM((4, 32, 128), F32),
        ],
        compiler_params=params(),
    )(cot, diag)


def fine_neighbours(ref, x, lo, hi):
    row = ref[x]
    mid = row[lo:hi]
    return (
        ref[x + 1, lo:hi] + ref[x - 1, lo:hi] + row[lo - 1 : hi - 1] + row[lo + 1 : hi + 1] + z_sum_fine(mid)
    )


def fine_down_kernel(
    f_ref, sg_ref, ylo_ref, yhi_ref, xlo_ref, xhi_ref, f2_ref, src_ref, gext_ref, fylo_ref, fyhi_ref, rhs_ref, s0, s1, pairs
):
    s0[2:10, 2:10] = sg_ref[0]
    s0[2:10, 0:2] = ylo_ref[0]
    s0[2:10, 10:12] = yhi_ref[0]
    s0[0:2] = xlo_ref[0]
    s0[10:12] = xhi_ref[0]
    gext_ref[2:10, 2:10] = sg_ref[1]
    gext_ref[2:10, 0:2] = ylo_ref[1]
    gext_ref[2:10, 10:12] = yhi_ref[1]
    gext_ref[0:2] = xlo_ref[1]
    gext_ref[10:12] = xhi_ref[1]

    def first(x, carry):
        total = fine_neighbours(s0, x, 1, 11)
        s1[x, 1:11] = THIRD * s0[x, 1:11] + gext_ref[x, 1:11] * total
        return carry

    lax.fori_loop(1, 11, first, 0)

    def second(x, carry):
        f1 = THIRD * f_ref[x - 2] + fine_neighbours(s0, x, 2, 10)
        f2_ref[x - 2] = THIRD * f1 + fine_neighbours(s1, x, 2, 10)
        src_ref[x - 2] = s0[x, 2:10] + s1[x, 2:10]
        return carry

    lax.fori_loop(2, 10, second, 0)
    fylo_ref[...] = f2_ref[:, 0:2]
    fyhi_ref[...] = f2_ref[:, 6:8]
    block_pairs(f2_ref, pairs)
    restrict_fine(pairs, rhs_ref, 1.0)


def fine_down(f, sg, ylo, yhi, xlo, xhi):
    return pl.pallas_call(
        fine_down_kernel,
        out_shape=(
            shape(8, 8, 8, 128),
            shape(8, 8, 8, 128),
            shape(12, 12, 8, 128),
            shape(8, 2, 8, 128),
            shape(8, 2, 8, 128),
            shape(4, 4, 4, 128),
        ),
        scratch_shapes=[
            pltpu.VMEM((12, 12, 8, 128), F32),
            pltpu.VMEM((12, 12, 8, 128), F32),
            pltpu.VMEM((4, 32, 128), F32),
        ],
        compiler_params=params(),
    )(f, sg, ylo, yhi, xlo, xhi)


def assemble_y(index_ref, blocks_ref, out_ref):
    me = index_ref[1]
    for k in range(8):
        source = lax.rem(me + (k + 4), 8)
        out_ref[:, :, 4 * k : 4 * k + 4, :] = blocks_ref[source]


def coefficients_kernel(index_ref, blocks_ref, g1_ref, c2_ref, field, pairs):
    assemble_y(index_ref, blocks_ref, field)
    g1_ref[...] = OMEGA / (6.0 + 4.0 * field[...])
    for x in range(2):
        row = field[4 + 2 * x] + field[5 + 2 * x]
        for c in range(2):
            pairs[x, c] = row[2 * c] + row[2 * c + 1]
            c2_ref[x, c] = 0.125 * (
                pairs[x, c, pl.ds(0, 16, stride=2), :] + pairs[x, c, pl.ds(1, 16, stride=2), :]
            )


def coefficients(index, blocks):
    return pl.pallas_call(
        coefficients_kernel,
        out_shape=(shape(12, 4, 32, 128), shape(2, 2, 16, 128)),
        in_specs=[smem(), vmem()],
        scratch_shapes=[pltpu.VMEM((12, 4, 32, 128), F32), pltpu.VMEM((2, 2, 32, 128), F32)],
        compiler_params=params(),
    )(index, blocks)


def middle_down_kernel(index_ref, blocks_ref, g_ref, f2_ref, src_ref, flo_ref, fhi_ref, rhs2_ref, rhs, s0, s1, pairs):
    assemble_y(index_ref, blocks_ref, rhs)
    s0[...] = g_ref[...] * rhs[...]

    def first(x, carry):
        total = coarse_neighbours(s0, x)
        s1[x] = THIRD * s0[x] + g_ref[x] * total
        rhs[x] = THIRD * rhs[x] + total
        return carry

    lax.fori_loop(1, 11, first, 0)

    def second(x, carry):
        f2_ref[x - 2] = THIRD * rhs[x] + coarse_neighbours(s1, x)
        src_ref[x - 2] = s0[x] + s1[x]
        return carry

    lax.fori_loop(2, 10, second, 0)
    flo_ref[...] = f2_ref[3]
    fhi_ref[...] = f2_ref[4]
    for x in range(2):
        row = f2_ref[2 + 2 * x] + f2_ref[3 + 2 * x]
        for c in range(2):
            pairs[x, c] = row[2 * c] + row[2 * c + 1]
            rhs2_ref[x, c] = pairs[x, c, pl.ds(0, 16, stride=2), :] + pairs[x, c, pl.ds(1, 16, stride=2), :]


def middle_down(index, blocks, g1):
    return pl.pallas_call(
        middle_down_kernel,
        out_shape=(
            shape(8, 4, 32, 128),
            shape(8, 4, 32, 128),
            shape(4, 32, 128),
            shape(4, 32, 128),
            shape(2, 2, 16, 128),
        ),
        in_specs=[smem(), vmem(), vmem()],
        scratch_shapes=[
            pltpu.VMEM((12, 4, 32, 128), F32),
            pltpu.VMEM((12, 4, 32, 128), F32),
            pltpu.VMEM((12, 4, 32, 128), F32),
            pltpu.VMEM((2, 2, 32, 128), F32),
        ],
        compiler_params=params(),
    )(index, blocks, g1)


def place_x(index_ref, pieces, out_ref):
    me = index_ref[0]
    z_me = lax.div(me, 4)
    step_y = 4 - 8 * lax.rem(lax.div(me, 2), 2)
    step_core = 2 - 4 * lax.rem(me, 2)
    offsets = (0, step_y, step_core, step_y + step_core)
    for piece, offset in zip(pieces, offsets):
        for k in range(8):
            source = lax.rem(z_me + (k + 4), 8)
            target = lax.rem(8 * k + offset + 64, 64)
            out_ref[pl.ds(target, 2)] = piece[source]


def up_kernel(
    index_ref, ra, rb, rc, rd, ca, cb, cc, cd, g1_ref, f1_ref, src1_ref, f1lo_ref, f1hi_ref,
    g0_ref, f0_ref, src0_ref, fylo_ref, fyhi_ref, fxlo_ref, fxhi_ref,
    guess_ref, source_ref,
    rhs2, g2, p2, q2, out3, e3, pairs3, win2, r2, sa2, out2, r1, sa1, out1, pairs1,
    rep, r0, f0, s3, s4, turned, placed,
):
    place_x(index_ref, (ra, rb, rc, rd), rhs2)
    place_x(index_ref, (ca, cb, cc, cd), g2)

    def restrict2(x, ref):
        row = ref[2 * x] + ref[2 * x + 1]
        pairs3[x] = row[0] + row[1]
        return pairs3[x, pl.ds(0, 8, stride=2), :] + pairs3[x, pl.ds(1, 8, stride=2), :]

    def scale2(x, carry):
        g3 = OMEGA / (6.0 + 64.0 * 0.125 * restrict2(x, g2))
        e3[1, x] = g3
        for r in range(2):
            row = 2 * x + r
            g = OMEGA / (6.0 + 16.0 * g2[row])
            g2[row] = g
            p2[row + 1] = g * rhs2[row]
        return carry

    lax.fori_loop(0, 32, scale2, 0)
    p2[0] = p2[64]
    p2[65] = p2[1]

    def first2(x, carry):
        total = coarse_neighbours(p2, x)
        q2[x] = THIRD * p2[x] + g2[x - 1] * total
        rhs2[x - 1] = THIRD * rhs2[x - 1] + total
        return carry

    lax.fori_loop(1, 65, first2, 0)
    q2[0] = q2[64]
    q2[65] = q2[1]

    def second2(x, carry):
        for r in range(2):
            row = 2 * x + r
            rhs2[row] = THIRD * rhs2[row] + coarse_neighbours(q2, row + 1)
        e3[0, x] = restrict2(x, rhs2)
        return carry

    lax.fori_loop(0, 32, second2, 0)

    g3 = e3[1]
    s = g3 * e3[0]
    acc = s
    for sweep in range(7):
        total = jnp.concatenate([s[1:], s[:1]], 0) + jnp.concatenate([s[31:], s[:31]], 0)
        total = total + pltpu.roll(s, 1, 1) + pltpu.roll(s, 7, 1)
        total = total + pltpu.roll(s, 1, 2) + pltpu.roll(s, 127, 2)
        s = THIRD * s + g3 * total
        acc = acc + s
    out3[...] = 0.5 * acc

    for x in range(10):
        half = out3[14 + x // 2]
        for c in range(2):
            r2[x, c, pl.ds(0, 8, stride=2), :] = half
            r2[x, c, pl.ds(1, 8, stride=2), :] = half
    for x in range(1, 9):
        g = g2[28 + x]
        f = rhs2[28 + x] - (OMEGA / g) * r2[x] + coarse_neighbours(r2, x)
        sa2[x] = g * f
    for x in range(2, 8):
        sb = THIRD * sa2[x] + g2[28 + x] * coarse_neighbours(sa2, x)
        out2[x - 2] = 0.5 * (p2[29 + x] + q2[29 + x] + r2[x] + sa2[x] + sb)

    for x in range(12):
        for c in range(4):
            half = out2[x // 2, c // 2]
            r1[x, c, pl.ds(0, 16, stride=2), :] = half
            r1[x, c, pl.ds(1, 16, stride=2), :] = half

    def residual1(x, f):
        g = g1_ref[x]
        sa1[x] = g * (f - (OMEGA / g) * r1[x] + coarse_neighbours(r1, x))

    residual1(1, f1lo_ref[...])
    residual1(10, f1hi_ref[...])

    def middle1(x, carry):
        residual1(x, f1_ref[x - 2])
        return carry

    lax.fori_loop(2, 10, middle1, 0)

    def last1(x, carry):
        sb = THIRD * sa1[x] + g1_ref[x] * coarse_neighbours(sa1, x)
        row = 0.5 * (src1_ref[x - 2] + r1[x] + sa1[x] + sb)
        for c in range(4):
            out1[x - 2, pl.ds(32 * c, 32), :] = row[c]
        return carry

    lax.fori_loop(2, 10, last1, 0)

    def spread0(x, carry):
        for y in range(8):
            row = out1[x, pl.ds(14 + y, 4, stride=32), :]
            rep[pl.ds(0, 4, stride=2), :] = row
            rep[pl.ds(1, 4, stride=2), :] = row
            both = rep[...]
            for p in range(2):
                for q in range(2):
                    r0[2 * x + p, 2 * y + q] = both
        return carry

    lax.fori_loop(0, 8, spread0, 0)
    f0[2:10, 2:10] = f0_ref[...]
    f0[2:10, 0:2] = fylo_ref[...]
    f0[2:10, 10:12] = fyhi_ref[...]
    f0[0:2] = fxlo_ref[...]
    f0[10:12] = fxhi_ref[...]

    def residual0(x, carry):
        g = g0_ref[x]
        f = f0[x] - (OMEGA / g) * r0[x + 2, 2:14] + fine_neighbours(r0, x + 2, 2, 14)
        f0[x] = f
        s3[x] = g * f
        return carry

    lax.fori_loop(0, 12, residual0, 0)

    def first0(x, carry):
        s4[x, 1:11] = THIRD * s3[x, 1:11] + g0_ref[x, 1:11] * fine_neighbours(s3, x, 1, 11)
        return carry

    lax.fori_loop(1, 11, first0, 0)

    def second0(x, carry):
        f4 = THIRD * f0[x, 2:10] + fine_neighbours(s3, x, 2, 10)
        f5 = THIRD * f4 + fine_neighbours(s4, x, 2, 10)
        source = src0_ref[x - 2] + r0[x + 2, 4:12] + s3[x, 2:10] + s4[x, 2:10]
        placed[pl.ds(64 * (x - 2), 64), :] = f5.reshape(64, 128)
        placed[pl.ds(64 * (x - 2) + 512, 64), :] = source.reshape(64, 128)
        return carry

    lax.fori_loop(2, 10, second0, 0)
    for c in range(8):
        turned[pl.ds(c, 128, stride=8), :] = placed[pl.ds(c, 128, stride=8), :].T
    result = turned[...].T
    guess_ref[...] = result[0:64].reshape(8, 8, 1024)
    source_ref[...] = result[64:128].reshape(8, 8, 1024)


def up(index, *arrays):
    scratch = [
        (64, 2, 16, 128), (64, 2, 16, 128), (66, 2, 16, 128), (66, 2, 16, 128),
        (32, 8, 128), (2, 32, 8, 128), (32, 16, 128), (8, 128),
        (10, 2, 16, 128), (10, 2, 16, 128), (6, 2, 16, 128),
        (12, 4, 32, 128), (12, 4, 32, 128), (8, 128, 128), (8, 128),
        (8, 128), (16, 16, 8, 128), (12, 12, 8, 128), (12, 12, 8, 128), (12, 12, 8, 128),
        (1024, 128), (1024, 128),
    ]
    return pl.pallas_call(
        up_kernel,
        out_shape=(shape(8, 8, 1024), shape(8, 8, 1024)),
        in_specs=[smem()] + [vmem()] * len(arrays),
        scratch_shapes=[pltpu.VMEM(dims, F32) for dims in scratch],
        compiler_params=params(),
    )(index, *arrays)


def shifted(v, axis, count, step):
    return lax.ppermute(v, axis, [(i, (i + step) % count) for i in range(count)])


def swapped(v, bit):
    return lax.ppermute(v, "gx", [(i, i ^ bit) for i in range(GX)])


def gather_y(v):
    return lax.all_to_all(jnp.broadcast_to(v[None], (GY,) + v.shape), "gy", 0, 0)


def with_x_blocks(v):
    before = shifted(v, "gx", GX, 1)
    after = shifted(v, "gx", GX, -1)
    return jnp.concatenate([before, v, after], axis=0)


def gather_x(v):
    groups = [[q + 4 * z for z in range(8)] for q in range(4)]
    along = lax.all_to_all(jnp.broadcast_to(v[None], (8,) + v.shape), "gx", 0, 0, axis_index_groups=groups)
    across = swapped(along, 2)
    return along, across, swapped(along, 1), swapped(across, 1)


def per_device(cotangent, diagonal):
    index = jnp.stack([lax.axis_index("gx"), lax.axis_index("gy")]).astype(jnp.int32)
    f, sg, ylo, yhi, c1 = prepare(cotangent, diagonal)

    ylo, yhi = shifted(yhi, "gy", GY, 1), shifted(ylo, "gy", GY, -1)
    xlo = jnp.concatenate([ylo[:, 0:2], sg[:, 0:2], yhi[:, 0:2]], axis=2)
    xhi = jnp.concatenate([ylo[:, 6:8], sg[:, 6:8], yhi[:, 6:8]], axis=2)
    xlo, xhi = shifted(xhi, "gx", GX, 1), shifted(xlo, "gx", GX, -1)

    g1, c2 = coefficients(index, gather_y(with_x_blocks(c1)))
    c2_pieces = gather_x(c2)

    f2, src0, g0, fylo, fyhi, rhs1 = fine_down(f, sg, ylo, yhi, xlo, xhi)
    fylo, fyhi = shifted(fyhi, "gy", GY, 1), shifted(fylo, "gy", GY, -1)
    fxlo = jnp.concatenate([fylo[0:2], f2[0:2], fyhi[0:2]], axis=1)
    fxhi = jnp.concatenate([fylo[6:8], f2[6:8], fyhi[6:8]], axis=1)
    fxlo, fxhi = shifted(fxhi, "gx", GX, 1), shifted(fxlo, "gx", GX, -1)

    f1, src1, f1lo, f1hi, rhs2 = middle_down(index, gather_y(with_x_blocks(rhs1)), g1)
    f1lo, f1hi = shifted(f1lo, "gx", GX, 1), shifted(f1hi, "gx", GX, -1)
    rhs2_pieces = gather_x(rhs2)

    return up(
        index, *rhs2_pieces, *c2_pieces, g1, f1, src1, f1lo, f1hi, g0, f2, src0, fylo, fyhi, fxlo, fxhi
    )


def solution(mesh):
    spec = P("gx", "gy", None)
    return jax.shard_map(per_device, mesh=mesh, in_specs=(spec, spec), out_specs=(spec, spec), check_vma=False)
```

```python
import jax
import jax.numpy as jnp
from jax import lax
from jax.experimental import pallas as pl
from jax.experimental.pallas import tpu as pltpu
from jax.sharding import PartitionSpec as P

GX = 32
GY = 8
OMEGA = 2.0 / 3.0
THIRD = 1.0 / 3.0
F32 = jnp.float32
VMEM_LIMIT = 48 * 1024 * 1024


def params():
    return pltpu.CompilerParams(vmem_limit_bytes=VMEM_LIMIT)


def shape(*dims):
    return jax.ShapeDtypeStruct(dims, F32)


def smem():
    return pl.BlockSpec(memory_space=pltpu.SMEM)


def vmem():
    return pl.BlockSpec(memory_space=pltpu.VMEM)


def z_sum_fine(v):
    last = v.ndim - 1
    place = lax.broadcasted_iota(jnp.int32, v.shape, last - 1)
    after = pltpu.roll(v, 7, last - 1)
    after = jnp.where(place == 7, pltpu.roll(after, 127, last), after)
    before = pltpu.roll(v, 1, last - 1)
    before = jnp.where(place == 0, pltpu.roll(before, 1, last), before)
    return after + before


def yz_sum(v):
    count, rows = v.shape[0], v.shape[1]
    total = pltpu.roll(v, 1, 1) + pltpu.roll(v, rows - 1, 1)
    parts = []
    for c in range(count):
        after = v[c + 1] if c < count - 1 else pltpu.roll(v[0], 127, 1)
        before = v[c - 1] if c > 0 else pltpu.roll(v[count - 1], 1, 1)
        parts.append(after + before)
    return total + jnp.stack(parts, 0)


def coarse_neighbours(ref, x):
    return ref[x + 1] + ref[x - 1] + yz_sum(ref[x])


def restrict_fine(pairs_ref, out_ref, scale):
    for x in range(4):
        for c in range(4):
            out_ref[x, c] = scale * (
                pairs_ref[x, pl.ds(2 * c, 4, stride=8), :] + pairs_ref[x, pl.ds(2 * c + 1, 4, stride=8), :]
            )


def block_pairs(field, pairs_ref):
    for x in range(4):
        row = field[2 * x] + field[2 * x + 1]
        for y in range(4):
            pairs_ref[x, pl.ds(8 * y, 8), :] = row[2 * y] + row[2 * y + 1]


def prepare_kernel(cot_ref, diag_ref, f_ref, sg_ref, ylo_ref, yhi_ref, c1_ref, turned, placed, pairs):
    stacked = jnp.concatenate([cot_ref[...].reshape(64, 1024), diag_ref[...].reshape(64, 1024)], axis=0)
    turned[...] = stacked.T
    for c in range(8):
        placed[pl.ds(c, 128, stride=8), :] = turned[pl.ds(c, 128, stride=8), :].T
    f = placed[0:512, :].reshape(8, 8, 8, 128)
    diag = placed[512:1024, :].reshape(8, 8, 8, 128)
    g = OMEGA / (6.0 + diag)
    s = g * f
    f_ref[...] = f
    sg_ref[0] = s
    sg_ref[1] = g
    ylo_ref[0] = s[:, 0:2]
    ylo_ref[1] = g[:, 0:2]
    yhi_ref[0] = s[:, 6:8]
    yhi_ref[1] = g[:, 6:8]
    block_pairs(diag, pairs)
    restrict_fine(pairs, c1_ref, 0.125)


def prepare(cot, diag):
    return pl.pallas_call(
        prepare_kernel,
        out_shape=(
            shape(8, 8, 8, 128),
            shape(2, 8, 8, 8, 128),
            shape(2, 8, 2, 8, 128),
            shape(2, 8, 2, 8, 128),
            shape(4, 4, 4, 128),
        ),
        scratch_shapes=[
            pltpu.VMEM((1024, 128), F32),
            pltpu.VMEM((1024, 128), F32),
            pltpu.VMEM((4, 32, 128), F32),
        ],
        compiler_params=params(),
    )(cot, diag)


def fine_neighbours(ref, x, lo, hi):
    row = ref[x]
    mid = row[lo:hi]
    return (
        ref[x + 1, lo:hi] + ref[x - 1, lo:hi] + row[lo - 1 : hi - 1] + row[lo + 1 : hi + 1] + z_sum_fine(mid)
    )


def fine_down_kernel(
    f_ref, sg_ref, ylo_ref, yhi_ref, xlo_ref, xhi_ref, f2_ref, src_ref, gext_ref, fylo_ref, fyhi_ref, rhs_ref, s0, s1, pairs
):
    s0[2:10, 2:10] = sg_ref[0]
    s0[2:10, 0:2] = ylo_ref[0]
    s0[2:10, 10:12] = yhi_ref[0]
    s0[0:2] = xlo_ref[0]
    s0[10:12] = xhi_ref[0]
    gext_ref[2:10, 2:10] = sg_ref[1]
    gext_ref[2:10, 0:2] = ylo_ref[1]
    gext_ref[2:10, 10:12] = yhi_ref[1]
    gext_ref[0:2] = xlo_ref[1]
    gext_ref[10:12] = xhi_ref[1]

    def first(x, carry):
        total = fine_neighbours(s0, x, 1, 11)
        s1[x, 1:11] = THIRD * s0[x, 1:11] + gext_ref[x, 1:11] * total
        return carry

    lax.fori_loop(1, 11, first, 0)

    def second(x, carry):
        f1 = THIRD * f_ref[x - 2] + fine_neighbours(s0, x, 2, 10)
        f2_ref[x - 2] = THIRD * f1 + fine_neighbours(s1, x, 2, 10)
        src_ref[x - 2] = s0[x, 2:10] + s1[x, 2:10]
        return carry

    lax.fori_loop(2, 10, second, 0)
    fylo_ref[...] = f2_ref[:, 0:2]
    fyhi_ref[...] = f2_ref[:, 6:8]
    block_pairs(f2_ref, pairs)
    restrict_fine(pairs, rhs_ref, 1.0)


def fine_down(f, sg, ylo, yhi, xlo, xhi):
    return pl.pallas_call(
        fine_down_kernel,
        out_shape=(
            shape(8, 8, 8, 128),
            shape(8, 8, 8, 128),
            shape(12, 12, 8, 128),
            shape(8, 2, 8, 128),
            shape(8, 2, 8, 128),
            shape(4, 4, 4, 128),
        ),
        scratch_shapes=[
            pltpu.VMEM((12, 12, 8, 128), F32),
            pltpu.VMEM((12, 12, 8, 128), F32),
            pltpu.VMEM((4, 32, 128), F32),
        ],
        compiler_params=params(),
    )(f, sg, ylo, yhi, xlo, xhi)


def core_of(index_ref):
    return lax.rem(index_ref[0], 2)


def assemble(index_ref, pieces, out_ref):
    core = core_of(index_ref)
    own, pair, outer, skip, far = pieces
    places = ((own, 6, 4), (pair, 10 - 8 * core, 4), (outer, 2 + 8 * core, 4), (skip, 14 * core, 2), (far, 14 - 14 * core, 2))
    for piece, base, count in places:
        for k in range(8):
            source = lax.rem(index_ref[1] + (k + 4), 8)
            out_ref[pl.ds(base, count), :, 4 * k : 4 * k + 4, :] = piece[source]


def restrict_middle(ref, x, pairs, scale):
    row = ref[x] + ref[x + 1]
    parts = []
    for c in range(2):
        pairs[c] = row[2 * c] + row[2 * c + 1]
        parts.append(scale * (pairs[c, pl.ds(0, 16, stride=2), :] + pairs[c, pl.ds(1, 16, stride=2), :]))
    return jnp.stack(parts, 0)


def restrict_coarse(upper, lower, pairs, scale):
    row = upper + lower
    pairs[0, 0:16] = row[0] + row[1]
    return scale * (pairs[0, pl.ds(0, 8, stride=2), :] + pairs[0, pl.ds(1, 8, stride=2), :])


def coefficients_kernel(index_ref, own, pair, outer, skip, far, g1_ref, g2_ref, c3_ref, field, c2, pairs):
    assemble(index_ref, (own, pair, outer, skip, far), field)

    def scale1(x, carry):
        g1_ref[x] = OMEGA / (6.0 + 4.0 * field[x])
        return carry

    lax.fori_loop(0, 16, scale1, 0)
    for x in range(8):
        c2[x] = restrict_middle(field, 2 * x, pairs, 0.125)
        g2_ref[x] = OMEGA / (6.0 + 16.0 * c2[x])
    c3_ref[...] = restrict_coarse(c2[3], c2[4], pairs, 0.125)


def coefficients(index, *pieces):
    return pl.pallas_call(
        coefficients_kernel,
        out_shape=(shape(16, 4, 32, 128), shape(8, 2, 16, 128), shape(8, 128)),
        in_specs=[smem()] + [vmem()] * 5,
        scratch_shapes=[pltpu.VMEM((16, 4, 32, 128), F32), pltpu.VMEM((8, 2, 16, 128), F32), pltpu.VMEM((2, 32, 128), F32)],
        compiler_params=params(),
    )(index, *pieces)


def middle_down_kernel(
    index_ref, own, pair, outer, skip, far, g1_ref, g2_ref, c3_ref,
    f1_ref, src1_ref, fs2_ref, part2_ref, both3_ref,
    rhs, s0, s1, f2, rhs2, t0, t1, pairs,
):
    assemble(index_ref, (own, pair, outer, skip, far), rhs)

    def start(x, carry):
        s0[x] = g1_ref[x] * rhs[x]
        return carry

    lax.fori_loop(0, 16, start, 0)

    def first(x, carry):
        total = coarse_neighbours(s0, x)
        s1[x] = THIRD * s0[x] + g1_ref[x] * total
        rhs[x] = THIRD * rhs[x] + total
        return carry

    lax.fori_loop(1, 15, first, 0)

    def second(x, carry):
        f2[x - 2] = THIRD * rhs[x] + coarse_neighbours(s1, x)
        return carry

    lax.fori_loop(2, 14, second, 0)
    f1_ref[...] = f2[1:11]
    src1_ref[...] = s0[4:12] + s1[4:12]

    for x in range(6):
        row = restrict_middle(f2, 2 * x, pairs, 1.0)
        rhs2[x] = row
        t0[x] = g2_ref[x + 1] * row
    for x in range(1, 5):
        total = coarse_neighbours(t0, x)
        t1[x] = THIRD * t0[x] + g2_ref[x + 1] * total
        rhs2[x] = THIRD * rhs2[x] + total
    for x in range(2, 4):
        fs2_ref[0, x - 2] = THIRD * rhs2[x] + coarse_neighbours(t1, x)
        fs2_ref[1, x - 2] = t0[x] + t1[x]
    part2_ref[...] = fs2_ref[0, 1 - core_of(index_ref)]
    both3_ref[0] = restrict_coarse(fs2_ref[0, 0], fs2_ref[0, 1], pairs, 1.0)
    both3_ref[1] = c3_ref[...]


def middle_down(index, pieces, g1, g2, c3):
    return pl.pallas_call(
        middle_down_kernel,
        out_shape=(
            shape(10, 4, 32, 128),
            shape(8, 4, 32, 128),
            shape(2, 2, 2, 16, 128),
            shape(2, 16, 128),
            shape(2, 8, 128),
        ),
        in_specs=[smem()] + [vmem()] * 8,
        scratch_shapes=[pltpu.VMEM((16, 4, 32, 128), F32)] * 3
        + [pltpu.VMEM((12, 4, 32, 128), F32)]
        + [pltpu.VMEM((6, 2, 16, 128), F32)] * 3
        + [pltpu.VMEM((2, 32, 128), F32)],
        compiler_params=params(),
    )(index, *pieces, g1, g2, c3)


def up_kernel(
    index_ref, mine3, other3, fs2, pair2, outer2, skip2, far2, g2_ref, g1_ref, f1_ref, src1_ref,
    g0_ref, f0_ref, src0_ref, fylo_ref, fyhi_ref, fxlo_ref, fxhi_ref,
    guess_ref, source_ref,
    e3, out3, f2, src2, r2, sa2, out2, r1, sa1, out1,
    rep, r0, f0, s3, s4, turned, placed,
):
    core = core_of(index_ref)
    chip = lax.div(index_ref[0], 2)

    for k in range(16):
        source = lax.rem(chip + (k + 8), 16)
        e3[2 * k + core] = mine3[source]
        e3[2 * k + 1 - core] = other3[source]
    g3 = OMEGA / (6.0 + 64.0 * e3[:, 1])
    s = g3 * e3[:, 0]
    acc = s
    for sweep in range(7):
        total = jnp.concatenate([s[1:], s[:1]], 0) + jnp.concatenate([s[31:], s[:31]], 0)
        total = total + pltpu.roll(s, 1, 1) + pltpu.roll(s, 7, 1)
        total = total + pltpu.roll(s, 1, 2) + pltpu.roll(s, 127, 2)
        s = THIRD * s + g3 * total
        acc = acc + s
    out3[...] = 0.5 * acc

    f2[2:4] = fs2[0]
    src2[2:4] = fs2[1]
    f2[pl.ds(4 - 4 * core, 2)] = pair2[0]
    src2[pl.ds(4 - 4 * core, 2)] = pair2[1]
    f2[pl.ds(4 * core, 2)] = outer2[0]
    src2[pl.ds(4 * core, 2)] = outer2[1]

    def row2(x):
        if x == 1:
            return jnp.where(core == 0, skip2[...], far2[...])
        if x == 8:
            return jnp.where(core == 0, far2[...], skip2[...])
        return f2[x - 2]

    for x in range(10):
        half = out3[14 + core + x // 2]
        for c in range(2):
            r2[x, c, pl.ds(0, 8, stride=2), :] = half
            r2[x, c, pl.ds(1, 8, stride=2), :] = half
    for x in range(1, 9):
        g = g2_ref[x - 1]
        sa2[x] = g * (row2(x) - (OMEGA / g) * r2[x] + coarse_neighbours(r2, x))
    for x in range(2, 8):
        sb = THIRD * sa2[x] + g2_ref[x - 1] * coarse_neighbours(sa2, x)
        out2[x - 2] = 0.5 * (src2[x - 2] + r2[x] + sa2[x] + sb)

    for x in range(12):
        for c in range(4):
            half = out2[x // 2, c // 2]
            r1[x, c, pl.ds(0, 16, stride=2), :] = half
            r1[x, c, pl.ds(1, 16, stride=2), :] = half

    def middle1(x, carry):
        g = g1_ref[x + 2]
        sa1[x] = g * (f1_ref[x - 1] - (OMEGA / g) * r1[x] + coarse_neighbours(r1, x))
        return carry

    lax.fori_loop(1, 11, middle1, 0)

    def last1(x, carry):
        sb = THIRD * sa1[x] + g1_ref[x + 2] * coarse_neighbours(sa1, x)
        row = 0.5 * (src1_ref[x - 2] + r1[x] + sa1[x] + sb)
        for c in range(4):
            out1[x - 2, pl.ds(32 * c, 32), :] = row[c]
        return carry

    lax.fori_loop(2, 10, last1, 0)

    def spread0(x, carry):
        for y in range(8):
            row = out1[x, pl.ds(14 + y, 4, stride=32), :]
            rep[pl.ds(0, 4, stride=2), :] = row
            rep[pl.ds(1, 4, stride=2), :] = row
            both = rep[...]
            for p in range(2):
                for q in range(2):
                    r0[2 * x + p, 2 * y + q] = both
        return carry

    lax.fori_loop(0, 8, spread0, 0)
    f0[2:10, 2:10] = f0_ref[...]
    f0[2:10, 0:2] = fylo_ref[...]
    f0[2:10, 10:12] = fyhi_ref[...]
    f0[0:2] = fxlo_ref[...]
    f0[10:12] = fxhi_ref[...]

    def residual0(x, carry):
        g = g0_ref[x]
        f = f0[x] - (OMEGA / g) * r0[x + 2, 2:14] + fine_neighbours(r0, x + 2, 2, 14)
        f0[x] = f
        s3[x] = g * f
        return carry

    lax.fori_loop(0, 12, residual0, 0)

    def first0(x, carry):
        s4[x, 1:11] = THIRD * s3[x, 1:11] + g0_ref[x, 1:11] * fine_neighbours(s3, x, 1, 11)
        return carry

    lax.fori_loop(1, 11, first0, 0)

    def second0(x, carry):
        f4 = THIRD * f0[x, 2:10] + fine_neighbours(s3, x, 2, 10)
        f5 = THIRD * f4 + fine_neighbours(s4, x, 2, 10)
        source = src0_ref[x - 2] + r0[x + 2, 4:12] + s3[x, 2:10] + s4[x, 2:10]
        placed[pl.ds(64 * (x - 2), 64), :] = f5.reshape(64, 128)
        placed[pl.ds(64 * (x - 2) + 512, 64), :] = source.reshape(64, 128)
        return carry

    lax.fori_loop(2, 10, second0, 0)
    for c in range(8):
        turned[pl.ds(c, 128, stride=8), :] = placed[pl.ds(c, 128, stride=8), :].T
    result = turned[...].T
    guess_ref[...] = result[0:64].reshape(8, 8, 1024)
    source_ref[...] = result[64:128].reshape(8, 8, 1024)


def up(index, *arrays):
    scratch = [
        (32, 2, 8, 128), (32, 8, 128), (6, 2, 16, 128), (6, 2, 16, 128),
        (10, 2, 16, 128), (10, 2, 16, 128), (6, 2, 16, 128),
        (12, 4, 32, 128), (12, 4, 32, 128), (8, 128, 128),
        (8, 128), (16, 16, 8, 128), (12, 12, 8, 128), (12, 12, 8, 128), (12, 12, 8, 128),
        (1024, 128), (1024, 128),
    ]
    return pl.pallas_call(
        up_kernel,
        out_shape=(shape(8, 8, 1024), shape(8, 8, 1024)),
        in_specs=[smem()] + [vmem()] * len(arrays),
        scratch_shapes=[pltpu.VMEM(dims, F32) for dims in scratch],
        compiler_params=params(),
    )(index, *arrays)


def shifted(v, axis, count, step):
    return lax.ppermute(v, axis, [(i, (i + step) % count) for i in range(count)])


def swap_core(v):
    return lax.ppermute(v, "gx", [(i, i ^ 1) for i in range(GX)])


def swap_outer(v):
    return lax.ppermute(v, "gx", [(i, (i + 1 if i % 2 else i - 1) % GX) for i in range(GX)])


def skip_chip(v):
    return lax.ppermute(v, "gx", [(i, (i - 2 if i % 2 else i + 2) % GX) for i in range(GX)])


def gather_y(v):
    return lax.all_to_all(jnp.broadcast_to(v[None], (GY,) + v.shape), "gy", 0, 0)


def level1_rows(core, v):
    pair = swap_core(v)
    outer = swap_outer(v)
    skip = skip_chip(jnp.where(core == 0, v[:, 2:4], v[:, 0:2]))
    far = swap_core(jnp.where(core == 0, outer[:, 2:4], outer[:, 0:2]))
    return v, pair, outer, skip, far


def per_device(cotangent, diagonal):
    core = lax.axis_index("gx") % 2
    index = jnp.stack([lax.axis_index("gx"), lax.axis_index("gy")]).astype(jnp.int32)
    f, sg, ylo, yhi, c1 = prepare(cotangent, diagonal)

    ylo, yhi = shifted(yhi, "gy", GY, 1), shifted(ylo, "gy", GY, -1)
    xlo = jnp.concatenate([ylo[:, 0:2], sg[:, 0:2], yhi[:, 0:2]], axis=2)
    xhi = jnp.concatenate([ylo[:, 6:8], sg[:, 6:8], yhi[:, 6:8]], axis=2)
    xlo, xhi = shifted(xhi, "gx", GX, 1), shifted(xlo, "gx", GX, -1)

    g1, g2, c3 = coefficients(index, *level1_rows(core, gather_y(c1)))

    f2, src0, g0, fylo, fyhi, rhs1 = fine_down(f, sg, ylo, yhi, xlo, xhi)
    fylo, fyhi = shifted(fyhi, "gy", GY, 1), shifted(fylo, "gy", GY, -1)
    fxlo = jnp.concatenate([fylo[0:2], f2[0:2], fyhi[0:2]], axis=1)
    fxhi = jnp.concatenate([fylo[6:8], f2[6:8], fyhi[6:8]], axis=1)
    fxlo, fxhi = shifted(fxhi, "gx", GX, 1), shifted(fxlo, "gx", GX, -1)

    f1, src1, fs2, part2, both3 = middle_down(index, level1_rows(core, gather_y(rhs1)), g1, g2, c3)
    pair2, outer2, skip2 = swap_core(fs2), swap_outer(fs2), skip_chip(part2)
    far2 = swap_core(jnp.where(core == 0, outer2[0, 1], outer2[0, 0]))

    groups = [[c + 2 * k for k in range(16)] for c in range(2)]
    mine3 = lax.all_to_all(jnp.broadcast_to(both3[None], (16,) + both3.shape), "gx", 0, 0, axis_index_groups=groups)
    other3 = swap_core(mine3)

    return up(
        index, mine3, other3, fs2, pair2, outer2, skip2, far2, g2, g1, f1, src1, g0, f2, src0, fylo, fyhi, fxlo, fxhi
    )


def solution(mesh):
    spec = P("gx", "gy", None)
    return jax.shard_map(per_device, mesh=mesh, in_specs=(spec, spec), out_specs=(spec, spec), check_vma=False)
```

```python
import jax
import jax.numpy as jnp
from jax import lax
from jax.experimental import pallas as pl
from jax.experimental.pallas import tpu as pltpu
from jax.sharding import PartitionSpec as P

GX = 32
GY = 8
OMEGA = 2.0 / 3.0
THIRD = 1.0 / 3.0
F32 = jnp.float32
VMEM_LIMIT = 48 * 1024 * 1024


def params():
    return pltpu.CompilerParams(vmem_limit_bytes=VMEM_LIMIT)


def shape(*dims):
    return jax.ShapeDtypeStruct(dims, F32)


def smem():
    return pl.BlockSpec(memory_space=pltpu.SMEM)


def vmem():
    return pl.BlockSpec(memory_space=pltpu.VMEM)


def z_sum_fine(v):
    last = v.ndim - 1
    place = lax.broadcasted_iota(jnp.int32, v.shape, last - 1)
    after = pltpu.roll(v, 7, last - 1)
    after = jnp.where(place == 7, pltpu.roll(after, 127, last), after)
    before = pltpu.roll(v, 1, last - 1)
    before = jnp.where(place == 0, pltpu.roll(before, 1, last), before)
    return after + before


def yz_sum(v):
    count, rows = v.shape[0], v.shape[1]
    total = pltpu.roll(v, 1, 1) + pltpu.roll(v, rows - 1, 1)
    parts = []
    for c in range(count):
        after = v[c + 1] if c < count - 1 else pltpu.roll(v[0], 127, 1)
        before = v[c - 1] if c > 0 else pltpu.roll(v[count - 1], 1, 1)
        parts.append(after + before)
    return total + jnp.stack(parts, 0)


def coarse_neighbours(ref, x):
    return ref[x + 1] + ref[x - 1] + yz_sum(ref[x])


def restrict_fine(pairs_ref, out_ref, scale):
    for x in range(4):
        for c in range(4):
            out_ref[x, c] = scale * (
                pairs_ref[x, pl.ds(2 * c, 4, stride=8), :] + pairs_ref[x, pl.ds(2 * c + 1, 4, stride=8), :]
            )


def block_pairs(field, pairs_ref):
    for x in range(4):
        row = field[2 * x] + field[2 * x + 1]
        for y in range(4):
            pairs_ref[x, pl.ds(8 * y, 8), :] = row[2 * y] + row[2 * y + 1]


def prepare_kernel(cot_ref, diag_ref, f_ref, sg_ref, ylo_ref, yhi_ref, c1_ref, stacked, turned, placed, pairs, sems):
    fetches = [
        pltpu.make_async_copy(ref.at[pl.ds(4 * h, 4)], stacked.at[k, pl.ds(4 * h, 4)], sems.at[k, h])
        for k, ref in enumerate((cot_ref, diag_ref))
        for h in range(2)
    ]
    for fetch in fetches:
        fetch.start()
    for fetch in fetches:
        fetch.wait()
    turned[...] = stacked[...].reshape(128, 1024).T
    for c in range(8):
        placed[pl.ds(c, 128, stride=8), :] = turned[pl.ds(c, 128, stride=8), :].T
    f = placed[0:512, :].reshape(8, 8, 8, 128)
    diag = placed[512:1024, :].reshape(8, 8, 8, 128)
    g = OMEGA / (6.0 + diag)
    s = g * f
    f_ref[...] = f
    sg_ref[0] = s
    sg_ref[1] = g
    ylo_ref[0] = s[:, 0:2]
    ylo_ref[1] = g[:, 0:2]
    yhi_ref[0] = s[:, 6:8]
    yhi_ref[1] = g[:, 6:8]
    block_pairs(diag, pairs)
    restrict_fine(pairs, c1_ref, 0.125)


def prepare(cot, diag):
    return pl.pallas_call(
        prepare_kernel,
        out_shape=(
            shape(8, 8, 8, 128),
            shape(2, 8, 8, 8, 128),
            shape(2, 8, 2, 8, 128),
            shape(2, 8, 2, 8, 128),
            shape(4, 4, 4, 128),
        ),
        in_specs=[pl.BlockSpec(memory_space=pl.ANY)] * 2,
        scratch_shapes=[
            pltpu.VMEM((2, 8, 8, 1024), F32),
            pltpu.VMEM((1024, 128), F32),
            pltpu.VMEM((1024, 128), F32),
            pltpu.VMEM((4, 32, 128), F32),
            pltpu.SemaphoreType.DMA((2, 2)),
        ],
        compiler_params=pltpu.CompilerParams(vmem_limit_bytes=62 * 1024 * 1024),
    )(cot, diag)


def fine_neighbours(ref, x, lo, hi):
    row = ref[x]
    mid = row[lo:hi]
    return (
        ref[x + 1, lo:hi] + ref[x - 1, lo:hi] + row[lo - 1 : hi - 1] + row[lo + 1 : hi + 1] + z_sum_fine(mid)
    )


def fine_down_kernel(
    f_ref, sg_ref, ylo_ref, yhi_ref, xlo_ref, xhi_ref, f2_ref, src_ref, gext_ref, fylo_ref, fyhi_ref, rhs_ref, s0, s1, pairs
):
    s0[2:10, 2:10] = sg_ref[0]
    s0[2:10, 0:2] = ylo_ref[0]
    s0[2:10, 10:12] = yhi_ref[0]
    s0[0:2] = xlo_ref[0]
    s0[10:12] = xhi_ref[0]
    gext_ref[2:10, 2:10] = sg_ref[1]
    gext_ref[2:10, 0:2] = ylo_ref[1]
    gext_ref[2:10, 10:12] = yhi_ref[1]
    gext_ref[0:2] = xlo_ref[1]
    gext_ref[10:12] = xhi_ref[1]

    def first(x, carry):
        total = fine_neighbours(s0, x, 1, 11)
        s1[x, 1:11] = THIRD * s0[x, 1:11] + gext_ref[x, 1:11] * total
        return carry

    lax.fori_loop(1, 11, first, 0, unroll=2)

    def second(x, carry):
        f1 = THIRD * f_ref[x - 2] + fine_neighbours(s0, x, 2, 10)
        f2_ref[x - 2] = THIRD * f1 + fine_neighbours(s1, x, 2, 10)
        src_ref[x - 2] = s0[x, 2:10] + s1[x, 2:10]
        return carry

    lax.fori_loop(2, 10, second, 0, unroll=2)
    fylo_ref[...] = f2_ref[:, 0:2]
    fyhi_ref[...] = f2_ref[:, 6:8]
    block_pairs(f2_ref, pairs)
    restrict_fine(pairs, rhs_ref, 1.0)


def fine_down(f, sg, ylo, yhi, xlo, xhi):
    return pl.pallas_call(
        fine_down_kernel,
        out_shape=(
            shape(8, 8, 8, 128),
            shape(8, 8, 8, 128),
            shape(12, 12, 8, 128),
            shape(8, 2, 8, 128),
            shape(8, 2, 8, 128),
            shape(4, 4, 4, 128),
        ),
        scratch_shapes=[
            pltpu.VMEM((12, 12, 8, 128), F32),
            pltpu.VMEM((12, 12, 8, 128), F32),
            pltpu.VMEM((4, 32, 128), F32),
        ],
        compiler_params=params(),
    )(f, sg, ylo, yhi, xlo, xhi)


def core_of(index_ref):
    return lax.rem(index_ref[0], 2)


def assemble(index_ref, pieces, out_ref):
    core = core_of(index_ref)
    own, pair, outer, skip, far = pieces
    places = ((own, 6, 4), (pair, 10 - 8 * core, 4), (outer, 2 + 8 * core, 4), (skip, 14 * core, 2), (far, 14 - 14 * core, 2))
    for piece, base, count in places:
        for k in range(8):
            source = lax.rem(index_ref[1] + (k + 4), 8)
            out_ref[pl.ds(base, count), :, 4 * k : 4 * k + 4, :] = piece[source]


def restrict_middle(ref, x, pairs, scale):
    row = ref[x] + ref[x + 1]
    parts = []
    for c in range(2):
        pairs[c] = row[2 * c] + row[2 * c + 1]
        parts.append(scale * (pairs[c, pl.ds(0, 16, stride=2), :] + pairs[c, pl.ds(1, 16, stride=2), :]))
    return jnp.stack(parts, 0)


def restrict_coarse(upper, lower, pairs, scale):
    row = upper + lower
    pairs[0, 0:16] = row[0] + row[1]
    return scale * (pairs[0, pl.ds(0, 8, stride=2), :] + pairs[0, pl.ds(1, 8, stride=2), :])


def coefficients_kernel(index_ref, own, pair, outer, skip, far, g1_ref, g2_ref, c3_ref, field, c2, pairs):
    assemble(index_ref, (own, pair, outer, skip, far), field)

    def scale1(x, carry):
        g1_ref[x] = OMEGA / (6.0 + 4.0 * field[x])
        return carry

    lax.fori_loop(0, 16, scale1, 0, unroll=2)
    for x in range(8):
        c2[x] = restrict_middle(field, 2 * x, pairs, 0.125)
        g2_ref[x] = OMEGA / (6.0 + 16.0 * c2[x])
    c3_ref[...] = restrict_coarse(c2[3], c2[4], pairs, 0.125)


def coefficients(index, *pieces):
    return pl.pallas_call(
        coefficients_kernel,
        out_shape=(shape(16, 4, 32, 128), shape(8, 2, 16, 128), shape(8, 128)),
        in_specs=[smem()] + [vmem()] * 5,
        scratch_shapes=[pltpu.VMEM((16, 4, 32, 128), F32), pltpu.VMEM((8, 2, 16, 128), F32), pltpu.VMEM((2, 32, 128), F32)],
        compiler_params=params(),
    )(index, *pieces)


def middle_down_kernel(
    index_ref, own, pair, outer, skip, far, g1_ref, g2_ref, c3_ref,
    f1_ref, src1_ref, fs2_ref, part2_ref, both3_ref,
    rhs, s0, s1, f2, rhs2, t0, t1, pairs,
):
    assemble(index_ref, (own, pair, outer, skip, far), rhs)

    def start(x, carry):
        s0[x] = g1_ref[x] * rhs[x]
        return carry

    lax.fori_loop(0, 16, start, 0, unroll=2)

    def first(x, carry):
        total = coarse_neighbours(s0, x)
        s1[x] = THIRD * s0[x] + g1_ref[x] * total
        rhs[x] = THIRD * rhs[x] + total
        return carry

    lax.fori_loop(1, 15, first, 0, unroll=2)

    def second(x, carry):
        f2[x - 2] = THIRD * rhs[x] + coarse_neighbours(s1, x)
        return carry

    lax.fori_loop(2, 14, second, 0, unroll=2)
    f1_ref[...] = f2[1:11]
    src1_ref[...] = s0[4:12] + s1[4:12]

    for x in range(6):
        row = restrict_middle(f2, 2 * x, pairs, 1.0)
        rhs2[x] = row
        t0[x] = g2_ref[x + 1] * row
    for x in range(1, 5):
        total = coarse_neighbours(t0, x)
        t1[x] = THIRD * t0[x] + g2_ref[x + 1] * total
        rhs2[x] = THIRD * rhs2[x] + total
    for x in range(2, 4):
        fs2_ref[0, x - 2] = THIRD * rhs2[x] + coarse_neighbours(t1, x)
        fs2_ref[1, x - 2] = t0[x] + t1[x]
    part2_ref[...] = fs2_ref[0, 1 - core_of(index_ref)]
    both3_ref[0] = restrict_coarse(fs2_ref[0, 0], fs2_ref[0, 1], pairs, 1.0)
    both3_ref[1] = c3_ref[...]


def middle_down(index, pieces, g1, g2, c3):
    return pl.pallas_call(
        middle_down_kernel,
        out_shape=(
            shape(10, 4, 32, 128),
            shape(8, 4, 32, 128),
            shape(2, 2, 2, 16, 128),
            shape(2, 16, 128),
            shape(2, 8, 128),
        ),
        in_specs=[smem()] + [vmem()] * 8,
        scratch_shapes=[pltpu.VMEM((16, 4, 32, 128), F32)] * 3
        + [pltpu.VMEM((12, 4, 32, 128), F32)]
        + [pltpu.VMEM((6, 2, 16, 128), F32)] * 3
        + [pltpu.VMEM((2, 32, 128), F32)],
        compiler_params=params(),
    )(index, *pieces, g1, g2, c3)


def up_kernel(
    index_ref, mine3, other3, fs2, pair2, outer2, skip2, far2, g2_ref, g1_ref, f1_ref, src1_ref,
    g0_ref, f0_ref, src0_ref, fylo_ref, fyhi_ref, fxlo_ref, fxhi_ref,
    guess_ref, source_ref,
    e3, out3, f2, src2, r2, sa2, out2, r1, sa1, out1,
    r0, f0, s3, s4, turned, placed,
):
    core = core_of(index_ref)
    chip = lax.div(index_ref[0], 2)

    for k in range(16):
        source = lax.rem(chip + (k + 8), 16)
        e3[2 * k + core] = mine3[source]
        e3[2 * k + 1 - core] = other3[source]
    g3 = OMEGA / (6.0 + 64.0 * e3[:, 1])
    s = g3 * e3[:, 0]
    acc = s
    for sweep in range(7):
        total = jnp.concatenate([s[1:], s[:1]], 0) + jnp.concatenate([s[31:], s[:31]], 0)
        total = total + pltpu.roll(s, 1, 1) + pltpu.roll(s, 7, 1)
        total = total + pltpu.roll(s, 1, 2) + pltpu.roll(s, 127, 2)
        s = THIRD * s + g3 * total
        acc = acc + s
    out3[...] = 0.5 * acc

    f2[2:4] = fs2[0]
    src2[2:4] = fs2[1]
    f2[pl.ds(4 - 4 * core, 2)] = pair2[0]
    src2[pl.ds(4 - 4 * core, 2)] = pair2[1]
    f2[pl.ds(4 * core, 2)] = outer2[0]
    src2[pl.ds(4 * core, 2)] = outer2[1]

    def row2(x):
        if x == 1:
            return jnp.where(core == 0, skip2[...], far2[...])
        if x == 8:
            return jnp.where(core == 0, far2[...], skip2[...])
        return f2[x - 2]

    for x in range(10):
        half = out3[14 + core + x // 2]
        for c in range(2):
            r2[x, c, pl.ds(0, 8, stride=2), :] = half
            r2[x, c, pl.ds(1, 8, stride=2), :] = half
    for x in range(1, 9):
        g = g2_ref[x - 1]
        sa2[x] = g * (row2(x) - (OMEGA / g) * r2[x] + coarse_neighbours(r2, x))
    for x in range(2, 8):
        sb = THIRD * sa2[x] + g2_ref[x - 1] * coarse_neighbours(sa2, x)
        out2[x - 2] = 0.5 * (src2[x - 2] + r2[x] + sa2[x] + sb)

    for x in range(12):
        for c in range(4):
            half = out2[x // 2, c // 2]
            r1[x, c, pl.ds(0, 16, stride=2), :] = half
            r1[x, c, pl.ds(1, 16, stride=2), :] = half

    def middle1(x, carry):
        g = g1_ref[x + 2]
        sa1[x] = g * (f1_ref[x - 1] - (OMEGA / g) * r1[x] + coarse_neighbours(r1, x))
        return carry

    lax.fori_loop(1, 11, middle1, 0, unroll=2)

    def last1(x, carry):
        sb = THIRD * sa1[x] + g1_ref[x + 2] * coarse_neighbours(sa1, x)
        row = 0.5 * (src1_ref[x - 2] + r1[x] + sa1[x] + sb)
        for c in range(4):
            out1[x - 2, pl.ds(32 * c, 32), :] = row[c]
        return carry

    lax.fori_loop(2, 10, last1, 0, unroll=2)

    def spread0(x, carry):
        for y in range(8):
            row = out1[x, pl.ds(14 + y, 4, stride=32), :]
            for p in range(2):
                for q in range(2):
                    for c in range(2):
                        r0[2 * x + p, 2 * y + q, pl.ds(c, 4, stride=2), :] = row
        return carry

    lax.fori_loop(0, 8, spread0, 0, unroll=2)
    f0[2:10, 2:10] = f0_ref[...]
    f0[2:10, 0:2] = fylo_ref[...]
    f0[2:10, 10:12] = fyhi_ref[...]
    f0[0:2] = fxlo_ref[...]
    f0[10:12] = fxhi_ref[...]

    def residual0(x, carry):
        g = g0_ref[x]
        f = f0[x] - (OMEGA / g) * r0[x + 2, 2:14] + fine_neighbours(r0, x + 2, 2, 14)
        f0[x] = f
        s3[x] = g * f
        return carry

    lax.fori_loop(0, 12, residual0, 0, unroll=2)

    def first0(x, carry):
        s4[x, 1:11] = THIRD * s3[x, 1:11] + g0_ref[x, 1:11] * fine_neighbours(s3, x, 1, 11)
        return carry

    lax.fori_loop(1, 11, first0, 0, unroll=2)

    def second0(x, carry):
        f4 = THIRD * f0[x, 2:10] + fine_neighbours(s3, x, 2, 10)
        f5 = THIRD * f4 + fine_neighbours(s4, x, 2, 10)
        source = src0_ref[x - 2] + r0[x + 2, 4:12] + s3[x, 2:10] + s4[x, 2:10]
        placed[pl.ds(64 * (x - 2), 64), :] = f5.reshape(64, 128)
        placed[pl.ds(64 * (x - 2) + 512, 64), :] = source.reshape(64, 128)
        return carry

    lax.fori_loop(2, 10, second0, 0, unroll=2)
    for c in range(8):
        turned[pl.ds(c, 128, stride=8), :] = placed[pl.ds(c, 128, stride=8), :].T
    result = turned[...].T
    guess_ref[...] = result[0:64].reshape(8, 8, 1024)
    source_ref[...] = result[64:128].reshape(8, 8, 1024)


def up(index, *arrays):
    scratch = [
        (32, 2, 8, 128), (32, 8, 128), (6, 2, 16, 128), (6, 2, 16, 128),
        (10, 2, 16, 128), (10, 2, 16, 128), (6, 2, 16, 128),
        (12, 4, 32, 128), (12, 4, 32, 128), (8, 128, 128),
        (16, 16, 8, 128), (12, 12, 8, 128), (12, 12, 8, 128), (12, 12, 8, 128),
        (1024, 128), (1024, 128),
    ]
    return pl.pallas_call(
        up_kernel,
        out_shape=(shape(8, 8, 1024), shape(8, 8, 1024)),
        in_specs=[smem()] + [vmem()] * len(arrays),
        scratch_shapes=[pltpu.VMEM(dims, F32) for dims in scratch],
        compiler_params=params(),
    )(index, *arrays)


def shifted(v, axis, count, step):
    return lax.ppermute(v, axis, [(i, (i + step) % count) for i in range(count)])


def swap_core(v):
    return lax.ppermute(v, "gx", [(i, i ^ 1) for i in range(GX)])


def swap_outer(v):
    return lax.ppermute(v, "gx", [(i, (i + 1 if i % 2 else i - 1) % GX) for i in range(GX)])


def skip_chip(v):
    return lax.ppermute(v, "gx", [(i, (i - 2 if i % 2 else i + 2) % GX) for i in range(GX)])


def gather_y(v):
    return lax.all_to_all(jnp.broadcast_to(v[None], (GY,) + v.shape), "gy", 0, 0)


def together(*arrays):
    return lax.optimization_barrier(arrays)


def level1_rows(core, v):
    pair = swap_core(v)
    outer = swap_outer(v)
    skip = skip_chip(jnp.where(core == 0, v[:, 2:4], v[:, 0:2]))
    pair, outer, skip = together(pair, outer, skip)
    far = swap_core(jnp.where(core == 0, outer[:, 2:4], outer[:, 0:2]))
    return v, pair, outer, skip, far


def per_device(cotangent, diagonal):
    core = lax.axis_index("gx") % 2
    index = jnp.stack([lax.axis_index("gx"), lax.axis_index("gy")]).astype(jnp.int32)
    f, sg, ylo, yhi, c1 = prepare(cotangent, diagonal)

    ylo, yhi = shifted(yhi, "gy", GY, 1), shifted(ylo, "gy", GY, -1)
    xlo = jnp.concatenate([ylo[:, 0:2], sg[:, 0:2], yhi[:, 0:2]], axis=2)
    xhi = jnp.concatenate([ylo[:, 6:8], sg[:, 6:8], yhi[:, 6:8]], axis=2)
    xlo, xhi = shifted(xhi, "gx", GX, 1), shifted(xlo, "gx", GX, -1)

    g1, g2, c3 = coefficients(index, *level1_rows(core, gather_y(c1)))

    f2, src0, g0, fylo, fyhi, rhs1 = fine_down(f, sg, ylo, yhi, xlo, xhi)
    fylo, fyhi = shifted(fyhi, "gy", GY, 1), shifted(fylo, "gy", GY, -1)
    fxlo = jnp.concatenate([fylo[0:2], f2[0:2], fyhi[0:2]], axis=1)
    fxhi = jnp.concatenate([fylo[6:8], f2[6:8], fyhi[6:8]], axis=1)
    fxlo, fxhi = shifted(fxhi, "gx", GX, 1), shifted(fxlo, "gx", GX, -1)

    f1, src1, fs2, part2, both3 = middle_down(index, level1_rows(core, gather_y(rhs1)), g1, g2, c3)
    pair2, outer2, skip2 = swap_core(fs2), swap_outer(fs2), skip_chip(part2)
    far2 = swap_core(jnp.where(core == 0, outer2[0, 1], outer2[0, 0]))

    groups = [[c + 2 * k for k in range(16)] for c in range(2)]
    mine3 = lax.all_to_all(jnp.broadcast_to(both3[None], (16,) + both3.shape), "gx", 0, 0, axis_index_groups=groups)
    other3 = swap_core(mine3)

    return up(
        index, mine3, other3, fs2, pair2, outer2, skip2, far2, g2, g1, f1, src1, g0, f2, src0, fylo, fyhi, fxlo, fxhi
    )


def solution(mesh):
    spec = P("gx", "gy", None)
    return jax.shard_map(per_device, mesh=mesh, in_specs=(spec, spec), out_specs=(spec, spec), check_vma=False)
```

```python
import jax
import jax.numpy as jnp
from jax import lax
from jax.experimental import pallas as pl
from jax.experimental.pallas import tpu as pltpu
from jax.sharding import PartitionSpec as P

GX = 32
GY = 8
OMEGA = 2.0 / 3.0
THIRD = 1.0 / 3.0
F32 = jnp.float32
VMEM_LIMIT = 48 * 1024 * 1024


def params():
    return pltpu.CompilerParams(vmem_limit_bytes=VMEM_LIMIT)


def shape(*dims):
    return jax.ShapeDtypeStruct(dims, F32)


def smem():
    return pl.BlockSpec(memory_space=pltpu.SMEM)


def vmem():
    return pl.BlockSpec(memory_space=pltpu.VMEM)


def z_sum_fine(v):
    last = v.ndim - 1
    place = lax.broadcasted_iota(jnp.int32, v.shape, last - 1)
    after = pltpu.roll(v, 7, last - 1)
    after = jnp.where(place == 7, pltpu.roll(after, 127, last), after)
    before = pltpu.roll(v, 1, last - 1)
    before = jnp.where(place == 0, pltpu.roll(before, 1, last), before)
    return after + before


def yz_sum(v):
    count, rows = v.shape[0], v.shape[1]
    total = pltpu.roll(v, 1, 1) + pltpu.roll(v, rows - 1, 1)
    parts = []
    for c in range(count):
        after = v[c + 1] if c < count - 1 else pltpu.roll(v[0], 127, 1)
        before = v[c - 1] if c > 0 else pltpu.roll(v[count - 1], 1, 1)
        parts.append(after + before)
    return total + jnp.stack(parts, 0)


def coarse_neighbours(ref, x):
    return ref[x + 1] + ref[x - 1] + yz_sum(ref[x])


def restrict_fine(pairs_ref, out_ref, scale):
    for x in range(4):
        for c in range(4):
            out_ref[x, c] = scale * (
                pairs_ref[x, pl.ds(2 * c, 4, stride=8), :] + pairs_ref[x, pl.ds(2 * c + 1, 4, stride=8), :]
            )


def block_pairs(field, pairs_ref):
    for x in range(4):
        row = field[2 * x] + field[2 * x + 1]
        for y in range(4):
            pairs_ref[x, pl.ds(8 * y, 8), :] = row[2 * y] + row[2 * y + 1]


def prepare_kernel(cot_ref, diag_ref, f_ref, sg_ref, ylo_ref, yhi_ref, c1_ref, turned, placed, pairs):
    stacked = jnp.concatenate([cot_ref[...].reshape(64, 1024), diag_ref[...].reshape(64, 1024)], axis=0)
    turned[...] = stacked.T
    for c in range(8):
        placed[pl.ds(c, 128, stride=8), :] = turned[pl.ds(c, 128, stride=8), :].T
    f = placed[0:512, :].reshape(8, 8, 8, 128)
    diag = placed[512:1024, :].reshape(8, 8, 8, 128)
    g = OMEGA / (6.0 + diag)
    s = g * f
    f_ref[...] = f
    sg_ref[0] = s
    sg_ref[1] = g
    ylo_ref[0] = s[:, 0:2]
    ylo_ref[1] = g[:, 0:2]
    yhi_ref[0] = s[:, 6:8]
    yhi_ref[1] = g[:, 6:8]
    block_pairs(diag, pairs)
    restrict_fine(pairs, c1_ref, 0.125)


def prepare(cot, diag):
    return pl.pallas_call(
        prepare_kernel,
        out_shape=(
            shape(8, 8, 8, 128),
            shape(2, 8, 8, 8, 128),
            shape(2, 8, 2, 8, 128),
            shape(2, 8, 2, 8, 128),
            shape(4, 4, 4, 128),
        ),
        scratch_shapes=[
            pltpu.VMEM((1024, 128), F32),
            pltpu.VMEM((1024, 128), F32),
            pltpu.VMEM((4, 32, 128), F32),
        ],
        compiler_params=params(),
    )(cot, diag)


def fine_neighbours(ref, x, lo, hi):
    row = ref[x]
    mid = row[lo:hi]
    return (
        ref[x + 1, lo:hi] + ref[x - 1, lo:hi] + row[lo - 1 : hi - 1] + row[lo + 1 : hi + 1] + z_sum_fine(mid)
    )


def fine_down_kernel(
    f_ref, sg_ref, ylo_ref, yhi_ref, xlo_ref, xhi_ref, f2_ref, src_ref, gext_ref, fylo_ref, fyhi_ref, rhs_ref, s0, s1, pairs
):
    s0[2:10, 2:10] = sg_ref[0]
    s0[2:10, 0:2] = ylo_ref[0]
    s0[2:10, 10:12] = yhi_ref[0]
    s0[0:2] = xlo_ref[0]
    s0[10:12] = xhi_ref[0]
    gext_ref[2:10, 2:10] = sg_ref[1]
    gext_ref[2:10, 0:2] = ylo_ref[1]
    gext_ref[2:10, 10:12] = yhi_ref[1]
    gext_ref[0:2] = xlo_ref[1]
    gext_ref[10:12] = xhi_ref[1]

    def first(x, carry):
        total = fine_neighbours(s0, x, 1, 11)
        s1[x, 1:11] = THIRD * s0[x, 1:11] + gext_ref[x, 1:11] * total
        return carry

    lax.fori_loop(1, 11, first, 0, unroll=4)

    def second(x, carry):
        f1 = THIRD * f_ref[x - 2] + fine_neighbours(s0, x, 2, 10)
        f2_ref[x - 2] = THIRD * f1 + fine_neighbours(s1, x, 2, 10)
        src_ref[x - 2] = s0[x, 2:10] + s1[x, 2:10]
        return carry

    lax.fori_loop(2, 10, second, 0, unroll=4)
    fylo_ref[...] = f2_ref[:, 0:2]
    fyhi_ref[...] = f2_ref[:, 6:8]
    block_pairs(f2_ref, pairs)
    restrict_fine(pairs, rhs_ref, 1.0)


def fine_down(f, sg, ylo, yhi, xlo, xhi):
    return pl.pallas_call(
        fine_down_kernel,
        out_shape=(
            shape(8, 8, 8, 128),
            shape(8, 8, 8, 128),
            shape(12, 12, 8, 128),
            shape(8, 2, 8, 128),
            shape(8, 2, 8, 128),
            shape(4, 4, 4, 128),
        ),
        scratch_shapes=[
            pltpu.VMEM((12, 12, 8, 128), F32),
            pltpu.VMEM((12, 12, 8, 128), F32),
            pltpu.VMEM((4, 32, 128), F32),
        ],
        compiler_params=params(),
    )(f, sg, ylo, yhi, xlo, xhi)


def core_of(index_ref):
    return lax.rem(index_ref[0], 2)


def assemble(index_ref, pieces, out_ref):
    core = core_of(index_ref)
    own, pair, outer, skip, far = pieces
    places = ((own, 6, 4), (pair, 10 - 8 * core, 4), (outer, 2 + 8 * core, 4), (skip, 14 * core, 2), (far, 14 - 14 * core, 2))
    for piece, base, count in places:
        for k in range(8):
            source = lax.rem(index_ref[1] + (k + 4), 8)
            out_ref[pl.ds(base, count), :, 4 * k : 4 * k + 4, :] = piece[source]


def restrict_middle(ref, x, pairs, scale):
    row = ref[x] + ref[x + 1]
    parts = []
    for c in range(2):
        pairs[c] = row[2 * c] + row[2 * c + 1]
        parts.append(scale * (pairs[c, pl.ds(0, 16, stride=2), :] + pairs[c, pl.ds(1, 16, stride=2), :]))
    return jnp.stack(parts, 0)


def restrict_coarse(upper, lower, pairs, scale):
    row = upper + lower
    pairs[0, 0:16] = row[0] + row[1]
    return scale * (pairs[0, pl.ds(0, 8, stride=2), :] + pairs[0, pl.ds(1, 8, stride=2), :])


def coefficients_kernel(index_ref, own, pair, outer, skip, far, g1_ref, g2_ref, c3_ref, field, c2, pairs):
    assemble(index_ref, (own, pair, outer, skip, far), field)

    def scale1(x, carry):
        g1_ref[x] = OMEGA / (6.0 + 4.0 * field[x])
        return carry

    lax.fori_loop(0, 16, scale1, 0, unroll=4)
    for x in range(8):
        c2[x] = restrict_middle(field, 2 * x, pairs, 0.125)
        g2_ref[x] = OMEGA / (6.0 + 16.0 * c2[x])
    c3_ref[...] = restrict_coarse(c2[3], c2[4], pairs, 0.125)


def coefficients(index, *pieces):
    return pl.pallas_call(
        coefficients_kernel,
        out_shape=(shape(16, 4, 32, 128), shape(8, 2, 16, 128), shape(8, 128)),
        in_specs=[smem()] + [vmem()] * 5,
        scratch_shapes=[pltpu.VMEM((16, 4, 32, 128), F32), pltpu.VMEM((8, 2, 16, 128), F32), pltpu.VMEM((2, 32, 128), F32)],
        compiler_params=params(),
    )(index, *pieces)


def middle_down_kernel(
    index_ref, own, pair, outer, skip, far, g1_ref, g2_ref, c3_ref,
    f1_ref, src1_ref, fs2_ref, part2_ref, both3_ref,
    rhs, s0, s1, f2, rhs2, t0, t1, pairs,
):
    assemble(index_ref, (own, pair, outer, skip, far), rhs)

    def start(x, carry):
        s0[x] = g1_ref[x] * rhs[x]
        return carry

    lax.fori_loop(0, 16, start, 0, unroll=4)

    def first(x, carry):
        total = coarse_neighbours(s0, x)
        s1[x] = THIRD * s0[x] + g1_ref[x] * total
        rhs[x] = THIRD * rhs[x] + total
        return carry

    lax.fori_loop(1, 15, first, 0, unroll=4)

    def second(x, carry):
        f2[x - 2] = THIRD * rhs[x] + coarse_neighbours(s1, x)
        return carry

    lax.fori_loop(2, 14, second, 0, unroll=4)
    f1_ref[...] = f2[1:11]
    src1_ref[...] = s0[4:12] + s1[4:12]

    for x in range(6):
        row = restrict_middle(f2, 2 * x, pairs, 1.0)
        rhs2[x] = row
        t0[x] = g2_ref[x + 1] * row
    for x in range(1, 5):
        total = coarse_neighbours(t0, x)
        t1[x] = THIRD * t0[x] + g2_ref[x + 1] * total
        rhs2[x] = THIRD * rhs2[x] + total
    for x in range(2, 4):
        fs2_ref[0, x - 2] = THIRD * rhs2[x] + coarse_neighbours(t1, x)
        fs2_ref[1, x - 2] = t0[x] + t1[x]
    part2_ref[...] = fs2_ref[0, 1 - core_of(index_ref)]
    both3_ref[0] = restrict_coarse(fs2_ref[0, 0], fs2_ref[0, 1], pairs, 1.0)
    both3_ref[1] = c3_ref[...]


def middle_down(index, pieces, g1, g2, c3):
    return pl.pallas_call(
        middle_down_kernel,
        out_shape=(
            shape(10, 4, 32, 128),
            shape(8, 4, 32, 128),
            shape(2, 2, 2, 16, 128),
            shape(2, 16, 128),
            shape(2, 8, 128),
        ),
        in_specs=[smem()] + [vmem()] * 8,
        scratch_shapes=[pltpu.VMEM((16, 4, 32, 128), F32)] * 3
        + [pltpu.VMEM((12, 4, 32, 128), F32)]
        + [pltpu.VMEM((6, 2, 16, 128), F32)] * 3
        + [pltpu.VMEM((2, 32, 128), F32)],
        compiler_params=params(),
    )(index, *pieces, g1, g2, c3)


def up_kernel(
    index_ref, mine3, other3, fs2, pair2, outer2, skip2, far2, g2_ref, g1_ref, f1_ref, src1_ref,
    g0_ref, f0_ref, src0_ref, fylo_ref, fyhi_ref, fxlo_ref, fxhi_ref,
    guess_ref, source_ref,
    e3, out3, f2, src2, r2, sa2, out2, r1, sa1, out1,
    r0, f0, s3, s4, turned, placed,
):
    core = core_of(index_ref)
    chip = lax.div(index_ref[0], 2)

    for k in range(16):
        source = lax.rem(chip + (k + 8), 16)
        e3[2 * k + core] = mine3[source]
        e3[2 * k + 1 - core] = other3[source]
    g3 = OMEGA / (6.0 + 64.0 * e3[:, 1])
    s = g3 * e3[:, 0]
    acc = s
    for sweep in range(7):
        total = jnp.concatenate([s[1:], s[:1]], 0) + jnp.concatenate([s[31:], s[:31]], 0)
        total = total + pltpu.roll(s, 1, 1) + pltpu.roll(s, 7, 1)
        total = total + pltpu.roll(s, 1, 2) + pltpu.roll(s, 127, 2)
        s = THIRD * s + g3 * total
        acc = acc + s
    out3[...] = 0.5 * acc

    f2[2:4] = fs2[0]
    src2[2:4] = fs2[1]
    f2[pl.ds(4 - 4 * core, 2)] = pair2[0]
    src2[pl.ds(4 - 4 * core, 2)] = pair2[1]
    f2[pl.ds(4 * core, 2)] = outer2[0]
    src2[pl.ds(4 * core, 2)] = outer2[1]

    def row2(x):
        if x == 1:
            return jnp.where(core == 0, skip2[...], far2[...])
        if x == 8:
            return jnp.where(core == 0, far2[...], skip2[...])
        return f2[x - 2]

    for x in range(10):
        half = out3[14 + core + x // 2]
        for c in range(2):
            r2[x, c, pl.ds(0, 8, stride=2), :] = half
            r2[x, c, pl.ds(1, 8, stride=2), :] = half
    for x in range(1, 9):
        g = g2_ref[x - 1]
        sa2[x] = g * (row2(x) - (OMEGA / g) * r2[x] + coarse_neighbours(r2, x))
    for x in range(2, 8):
        sb = THIRD * sa2[x] + g2_ref[x - 1] * coarse_neighbours(sa2, x)
        out2[x - 2] = 0.5 * (src2[x - 2] + r2[x] + sa2[x] + sb)

    for x in range(12):
        for c in range(4):
            half = out2[x // 2, c // 2]
            r1[x, c, pl.ds(0, 16, stride=2), :] = half
            r1[x, c, pl.ds(1, 16, stride=2), :] = half

    def middle1(x, carry):
        g = g1_ref[x + 2]
        sa1[x] = g * (f1_ref[x - 1] - (OMEGA / g) * r1[x] + coarse_neighbours(r1, x))
        return carry

    lax.fori_loop(1, 11, middle1, 0, unroll=4)

    def last1(x, carry):
        sb = THIRD * sa1[x] + g1_ref[x + 2] * coarse_neighbours(sa1, x)
        row = 0.5 * (src1_ref[x - 2] + r1[x] + sa1[x] + sb)
        for c in range(4):
            out1[x - 2, pl.ds(32 * c, 32), :] = row[c]
        return carry

    lax.fori_loop(2, 10, last1, 0, unroll=4)

    def spread0(x, carry):
        for y in range(8):
            row = out1[x, pl.ds(14 + y, 4, stride=32), :]
            for p in range(2):
                for q in range(2):
                    for c in range(2):
                        r0[2 * x + p, 2 * y + q, pl.ds(c, 4, stride=2), :] = row
        return carry

    lax.fori_loop(0, 8, spread0, 0, unroll=4)
    f0[2:10, 2:10] = f0_ref[...]
    f0[2:10, 0:2] = fylo_ref[...]
    f0[2:10, 10:12] = fyhi_ref[...]
    f0[0:2] = fxlo_ref[...]
    f0[10:12] = fxhi_ref[...]

    def residual0(x, carry):
        g = g0_ref[x]
        f = f0[x] - (OMEGA / g) * r0[x + 2, 2:14] + fine_neighbours(r0, x + 2, 2, 14)
        f0[x] = f
        s3[x] = g * f
        return carry

    lax.fori_loop(0, 12, residual0, 0, unroll=4)

    def first0(x, carry):
        s4[x, 1:11] = THIRD * s3[x, 1:11] + g0_ref[x, 1:11] * fine_neighbours(s3, x, 1, 11)
        return carry

    lax.fori_loop(1, 11, first0, 0, unroll=4)

    def second0(x, carry):
        f4 = THIRD * f0[x, 2:10] + fine_neighbours(s3, x, 2, 10)
        f5 = THIRD * f4 + fine_neighbours(s4, x, 2, 10)
        source = src0_ref[x - 2] + r0[x + 2, 4:12] + s3[x, 2:10] + s4[x, 2:10]
        placed[pl.ds(64 * (x - 2), 64), :] = f5.reshape(64, 128)
        placed[pl.ds(64 * (x - 2) + 512, 64), :] = source.reshape(64, 128)
        return carry

    lax.fori_loop(2, 10, second0, 0, unroll=4)
    for c in range(8):
        turned[pl.ds(c, 128, stride=8), :] = placed[pl.ds(c, 128, stride=8), :].T
    result = turned[...].T
    guess_ref[...] = result[0:64].reshape(8, 8, 1024)
    source_ref[...] = result[64:128].reshape(8, 8, 1024)


def up(index, *arrays):
    scratch = [
        (32, 2, 8, 128), (32, 8, 128), (6, 2, 16, 128), (6, 2, 16, 128),
        (10, 2, 16, 128), (10, 2, 16, 128), (6, 2, 16, 128),
        (12, 4, 32, 128), (12, 4, 32, 128), (8, 128, 128),
        (16, 16, 8, 128), (12, 12, 8, 128), (12, 12, 8, 128), (12, 12, 8, 128),
        (1024, 128), (1024, 128),
    ]
    return pl.pallas_call(
        up_kernel,
        out_shape=(shape(8, 8, 1024), shape(8, 8, 1024)),
        in_specs=[smem()] + [vmem()] * len(arrays),
        scratch_shapes=[pltpu.VMEM(dims, F32) for dims in scratch],
        compiler_params=params(),
    )(index, *arrays)


def shifted(v, axis, count, step):
    return lax.ppermute(v, axis, [(i, (i + step) % count) for i in range(count)])


def swap_core(v):
    return lax.ppermute(v, "gx", [(i, i ^ 1) for i in range(GX)])


def swap_outer(v):
    return lax.ppermute(v, "gx", [(i, (i + 1 if i % 2 else i - 1) % GX) for i in range(GX)])


def skip_chip(v):
    return lax.ppermute(v, "gx", [(i, (i - 2 if i % 2 else i + 2) % GX) for i in range(GX)])


def gather_y(v):
    return lax.all_to_all(jnp.broadcast_to(v[None], (GY,) + v.shape), "gy", 0, 0)


def together(*arrays):
    return lax.optimization_barrier(arrays)


def level1_rows(core, v):
    pair = swap_core(v)
    outer = swap_outer(v)
    skip = skip_chip(jnp.where(core == 0, v[:, 2:4], v[:, 0:2]))
    pair, outer, skip = together(pair, outer, skip)
    far = swap_core(jnp.where(core == 0, outer[:, 2:4], outer[:, 0:2]))
    return v, pair, outer, skip, far


def per_device(cotangent, diagonal):
    core = lax.axis_index("gx") % 2
    index = jnp.stack([lax.axis_index("gx"), lax.axis_index("gy")]).astype(jnp.int32)
    f, sg, ylo, yhi, c1 = prepare(cotangent, diagonal)

    ylo, yhi = shifted(yhi, "gy", GY, 1), shifted(ylo, "gy", GY, -1)
    xlo = jnp.concatenate([ylo[:, 0:2], sg[:, 0:2], yhi[:, 0:2]], axis=2)
    xhi = jnp.concatenate([ylo[:, 6:8], sg[:, 6:8], yhi[:, 6:8]], axis=2)
    xlo, xhi = shifted(xhi, "gx", GX, 1), shifted(xlo, "gx", GX, -1)

    g1, g2, c3 = coefficients(index, *level1_rows(core, gather_y(c1)))

    f2, src0, g0, fylo, fyhi, rhs1 = fine_down(f, sg, ylo, yhi, xlo, xhi)
    fylo, fyhi = shifted(fyhi, "gy", GY, 1), shifted(fylo, "gy", GY, -1)
    fxlo = jnp.concatenate([fylo[0:2], f2[0:2], fyhi[0:2]], axis=1)
    fxhi = jnp.concatenate([fylo[6:8], f2[6:8], fyhi[6:8]], axis=1)
    fxlo, fxhi = shifted(fxhi, "gx", GX, 1), shifted(fxlo, "gx", GX, -1)

    f1, src1, fs2, part2, both3 = middle_down(index, level1_rows(core, gather_y(rhs1)), g1, g2, c3)
    pair2, outer2, skip2 = swap_core(fs2), swap_outer(fs2), skip_chip(part2)
    far2 = swap_core(jnp.where(core == 0, outer2[0, 1], outer2[0, 0]))

    groups = [[c + 2 * k for k in range(16)] for c in range(2)]
    mine3 = lax.all_to_all(jnp.broadcast_to(both3[None], (16,) + both3.shape), "gx", 0, 0, axis_index_groups=groups)
    other3 = swap_core(mine3)

    return up(
        index, mine3, other3, fs2, pair2, outer2, skip2, far2, g2, g1, f1, src1, g0, f2, src0, fylo, fyhi, fxlo, fxhi
    )


def solution(mesh):
    spec = P("gx", "gy", None)
    return jax.shard_map(per_device, mesh=mesh, in_specs=(spec, spec), out_specs=(spec, spec), check_vma=False)
```

```python
import jax
import jax.numpy as jnp
from jax import lax
from jax.experimental import pallas as pl
from jax.experimental.pallas import tpu as pltpu
from jax.sharding import PartitionSpec as P

GX = 32
GY = 8
OMEGA = 2.0 / 3.0
THIRD = 1.0 / 3.0
F32 = jnp.float32
VMEM_LIMIT = 48 * 1024 * 1024


def params():
    return pltpu.CompilerParams(vmem_limit_bytes=VMEM_LIMIT)


def shape(*dims):
    return jax.ShapeDtypeStruct(dims, F32)


def smem():
    return pl.BlockSpec(memory_space=pltpu.SMEM)


def vmem():
    return pl.BlockSpec(memory_space=pltpu.VMEM)


def z_sum_fine(v):
    last = v.ndim - 1
    place = lax.broadcasted_iota(jnp.int32, v.shape, last - 1)
    after = pltpu.roll(v, 7, last - 1)
    after = jnp.where(place == 7, pltpu.roll(after, 127, last), after)
    before = pltpu.roll(v, 1, last - 1)
    before = jnp.where(place == 0, pltpu.roll(before, 1, last), before)
    return after + before


def yz_sum(v):
    count, rows = v.shape[0], v.shape[1]
    total = pltpu.roll(v, 1, 1) + pltpu.roll(v, rows - 1, 1)
    parts = []
    for c in range(count):
        after = v[c + 1] if c < count - 1 else pltpu.roll(v[0], 127, 1)
        before = v[c - 1] if c > 0 else pltpu.roll(v[count - 1], 1, 1)
        parts.append(after + before)
    return total + jnp.stack(parts, 0)


def coarse_neighbours(ref, x):
    return ref[x + 1] + ref[x - 1] + yz_sum(ref[x])


def restrict_fine(pairs_ref, out_ref, scale):
    for x in range(4):
        for c in range(4):
            out_ref[x, c] = scale * (
                pairs_ref[x, pl.ds(2 * c, 4, stride=8), :] + pairs_ref[x, pl.ds(2 * c + 1, 4, stride=8), :]
            )


def block_pairs(field, pairs_ref):
    for x in range(4):
        row = field[2 * x] + field[2 * x + 1]
        for y in range(4):
            pairs_ref[x, pl.ds(8 * y, 8), :] = row[2 * y] + row[2 * y + 1]


def prepare_kernel(cot_ref, diag_ref, f_ref, sg_ref, ylo_ref, yhi_ref, c1_ref, turned, placed, pairs):
    stacked = jnp.concatenate([cot_ref[...].reshape(64, 1024), diag_ref[...].reshape(64, 1024)], axis=0)
    turned[...] = stacked.T
    for c in range(8):
        placed[pl.ds(c, 128, stride=8), :] = turned[pl.ds(c, 128, stride=8), :].T
    f = placed[0:512, :].reshape(8, 8, 8, 128)
    diag = placed[512:1024, :].reshape(8, 8, 8, 128)
    g = OMEGA / (6.0 + diag)
    s = g * f
    f_ref[...] = f
    sg_ref[0] = s
    sg_ref[1] = g
    ylo_ref[0] = s[:, 0:2]
    ylo_ref[1] = g[:, 0:2]
    yhi_ref[0] = s[:, 6:8]
    yhi_ref[1] = g[:, 6:8]
    block_pairs(diag, pairs)
    restrict_fine(pairs, c1_ref, 0.125)


def prepare(cot, diag):
    return pl.pallas_call(
        prepare_kernel,
        out_shape=(
            shape(8, 8, 8, 128),
            shape(2, 8, 8, 8, 128),
            shape(2, 8, 2, 8, 128),
            shape(2, 8, 2, 8, 128),
            shape(4, 4, 4, 128),
        ),
        scratch_shapes=[
            pltpu.VMEM((1024, 128), F32),
            pltpu.VMEM((1024, 128), F32),
            pltpu.VMEM((4, 32, 128), F32),
        ],
        compiler_params=params(),
    )(cot, diag)


def fine_neighbours(ref, x, lo, hi):
    row = ref[x]
    mid = row[lo:hi]
    return (
        ref[x + 1, lo:hi] + ref[x - 1, lo:hi] + row[lo - 1 : hi - 1] + row[lo + 1 : hi + 1] + z_sum_fine(mid)
    )


def fine_down_kernel(
    f_ref, sg_ref, ylo_ref, yhi_ref, xlo_ref, xhi_ref, f2_ref, src_ref, gext_ref, fylo_ref, fyhi_ref, rhs_ref, s0, s1, pairs
):
    s0[2:10, 2:10] = sg_ref[0]
    s0[2:10, 0:2] = ylo_ref[0]
    s0[2:10, 10:12] = yhi_ref[0]
    s0[0:2] = xlo_ref[0]
    s0[10:12] = xhi_ref[0]
    gext_ref[2:10, 2:10] = sg_ref[1]
    gext_ref[2:10, 0:2] = ylo_ref[1]
    gext_ref[2:10, 10:12] = yhi_ref[1]
    gext_ref[0:2] = xlo_ref[1]
    gext_ref[10:12] = xhi_ref[1]

    def first(x, carry):
        total = fine_neighbours(s0, x, 1, 11)
        s1[x, 1:11] = THIRD * s0[x, 1:11] + gext_ref[x, 1:11] * total
        return carry

    lax.fori_loop(1, 11, first, 0, unroll=8)

    def second(x, carry):
        f1 = THIRD * f_ref[x - 2] + fine_neighbours(s0, x, 2, 10)
        f2_ref[x - 2] = THIRD * f1 + fine_neighbours(s1, x, 2, 10)
        src_ref[x - 2] = s0[x, 2:10] + s1[x, 2:10]
        return carry

    lax.fori_loop(2, 10, second, 0, unroll=8)
    fylo_ref[...] = f2_ref[:, 0:2]
    fyhi_ref[...] = f2_ref[:, 6:8]
    block_pairs(f2_ref, pairs)
    restrict_fine(pairs, rhs_ref, 1.0)


def fine_down(f, sg, ylo, yhi, xlo, xhi):
    return pl.pallas_call(
        fine_down_kernel,
        out_shape=(
            shape(8, 8, 8, 128),
            shape(8, 8, 8, 128),
            shape(12, 12, 8, 128),
            shape(8, 2, 8, 128),
            shape(8, 2, 8, 128),
            shape(4, 4, 4, 128),
        ),
        scratch_shapes=[
            pltpu.VMEM((12, 12, 8, 128), F32),
            pltpu.VMEM((12, 12, 8, 128), F32),
            pltpu.VMEM((4, 32, 128), F32),
        ],
        compiler_params=params(),
    )(f, sg, ylo, yhi, xlo, xhi)


def core_of(index_ref):
    return lax.rem(index_ref[0], 2)


def assemble(index_ref, pieces, out_ref):
    core = core_of(index_ref)
    own, pair, outer, skip, far = pieces
    places = ((own, 6, 4), (pair, 10 - 8 * core, 4), (outer, 2 + 8 * core, 4), (skip, 14 * core, 2), (far, 14 - 14 * core, 2))
    for piece, base, count in places:
        for k in range(8):
            source = lax.rem(index_ref[1] + (k + 4), 8)
            out_ref[pl.ds(base, count), :, 4 * k : 4 * k + 4, :] = piece[source]


def restrict_middle(ref, x, pairs, scale):
    row = ref[x] + ref[x + 1]
    parts = []
    for c in range(2):
        pairs[c] = row[2 * c] + row[2 * c + 1]
        parts.append(scale * (pairs[c, pl.ds(0, 16, stride=2), :] + pairs[c, pl.ds(1, 16, stride=2), :]))
    return jnp.stack(parts, 0)


def restrict_coarse(upper, lower, pairs, scale):
    row = upper + lower
    pairs[0, 0:16] = row[0] + row[1]
    return scale * (pairs[0, pl.ds(0, 8, stride=2), :] + pairs[0, pl.ds(1, 8, stride=2), :])


def coefficients_kernel(index_ref, own, pair, outer, skip, far, g1_ref, g2_ref, c3_ref, field, c2, pairs):
    assemble(index_ref, (own, pair, outer, skip, far), field)

    def scale1(x, carry):
        g1_ref[x] = OMEGA / (6.0 + 4.0 * field[x])
        return carry

    lax.fori_loop(0, 16, scale1, 0, unroll=8)
    for x in range(8):
        c2[x] = restrict_middle(field, 2 * x, pairs, 0.125)
        g2_ref[x] = OMEGA / (6.0 + 16.0 * c2[x])
    c3_ref[...] = restrict_coarse(c2[3], c2[4], pairs, 0.125)


def coefficients(index, *pieces):
    return pl.pallas_call(
        coefficients_kernel,
        out_shape=(shape(16, 4, 32, 128), shape(8, 2, 16, 128), shape(8, 128)),
        in_specs=[smem()] + [vmem()] * 5,
        scratch_shapes=[pltpu.VMEM((16, 4, 32, 128), F32), pltpu.VMEM((8, 2, 16, 128), F32), pltpu.VMEM((2, 32, 128), F32)],
        compiler_params=params(),
    )(index, *pieces)


def middle_down_kernel(
    index_ref, own, pair, outer, skip, far, g1_ref, g2_ref, c3_ref,
    f1_ref, src1_ref, fs2_ref, part2_ref, both3_ref,
    rhs, s0, s1, f2, rhs2, t0, t1, pairs,
):
    assemble(index_ref, (own, pair, outer, skip, far), rhs)

    def start(x, carry):
        s0[x] = g1_ref[x] * rhs[x]
        return carry

    lax.fori_loop(0, 16, start, 0, unroll=8)

    def first(x, carry):
        total = coarse_neighbours(s0, x)
        s1[x] = THIRD * s0[x] + g1_ref[x] * total
        rhs[x] = THIRD * rhs[x] + total
        return carry

    lax.fori_loop(1, 15, first, 0, unroll=8)

    def second(x, carry):
        f2[x - 2] = THIRD * rhs[x] + coarse_neighbours(s1, x)
        return carry

    lax.fori_loop(2, 14, second, 0, unroll=8)
    f1_ref[...] = f2[1:11]
    src1_ref[...] = s0[4:12] + s1[4:12]

    for x in range(6):
        row = restrict_middle(f2, 2 * x, pairs, 1.0)
        rhs2[x] = row
        t0[x] = g2_ref[x + 1] * row
    for x in range(1, 5):
        total = coarse_neighbours(t0, x)
        t1[x] = THIRD * t0[x] + g2_ref[x + 1] * total
        rhs2[x] = THIRD * rhs2[x] + total
    for x in range(2, 4):
        fs2_ref[0, x - 2] = THIRD * rhs2[x] + coarse_neighbours(t1, x)
        fs2_ref[1, x - 2] = t0[x] + t1[x]
    part2_ref[...] = fs2_ref[0, 1 - core_of(index_ref)]
    both3_ref[0] = restrict_coarse(fs2_ref[0, 0], fs2_ref[0, 1], pairs, 1.0)
    both3_ref[1] = c3_ref[...]


def middle_down(index, pieces, g1, g2, c3):
    return pl.pallas_call(
        middle_down_kernel,
        out_shape=(
            shape(10, 4, 32, 128),
            shape(8, 4, 32, 128),
            shape(2, 2, 2, 16, 128),
            shape(2, 16, 128),
            shape(2, 8, 128),
        ),
        in_specs=[smem()] + [vmem()] * 8,
        scratch_shapes=[pltpu.VMEM((16, 4, 32, 128), F32)] * 3
        + [pltpu.VMEM((12, 4, 32, 128), F32)]
        + [pltpu.VMEM((6, 2, 16, 128), F32)] * 3
        + [pltpu.VMEM((2, 32, 128), F32)],
        compiler_params=params(),
    )(index, *pieces, g1, g2, c3)


def up_kernel(
    index_ref, mine3, other3, fs2, pair2, outer2, skip2, far2, g2_ref, g1_ref, f1_ref, src1_ref,
    g0_ref, f0_ref, src0_ref, fylo_ref, fyhi_ref, fxlo_ref, fxhi_ref,
    guess_ref, source_ref,
    e3, out3, f2, src2, r2, sa2, out2, r1, sa1, out1,
    r0, f0, s3, s4, turned, placed,
):
    core = core_of(index_ref)
    chip = lax.div(index_ref[0], 2)

    for k in range(16):
        source = lax.rem(chip + (k + 8), 16)
        e3[2 * k + core] = mine3[source]
        e3[2 * k + 1 - core] = other3[source]
    g3 = OMEGA / (6.0 + 64.0 * e3[:, 1])
    s = g3 * e3[:, 0]
    acc = s
    for sweep in range(7):
        total = jnp.concatenate([s[1:], s[:1]], 0) + jnp.concatenate([s[31:], s[:31]], 0)
        total = total + pltpu.roll(s, 1, 1) + pltpu.roll(s, 7, 1)
        total = total + pltpu.roll(s, 1, 2) + pltpu.roll(s, 127, 2)
        s = THIRD * s + g3 * total
        acc = acc + s
    out3[...] = 0.5 * acc

    f2[2:4] = fs2[0]
    src2[2:4] = fs2[1]
    f2[pl.ds(4 - 4 * core, 2)] = pair2[0]
    src2[pl.ds(4 - 4 * core, 2)] = pair2[1]
    f2[pl.ds(4 * core, 2)] = outer2[0]
    src2[pl.ds(4 * core, 2)] = outer2[1]

    def row2(x):
        if x == 1:
            return jnp.where(core == 0, skip2[...], far2[...])
        if x == 8:
            return jnp.where(core == 0, far2[...], skip2[...])
        return f2[x - 2]

    for x in range(10):
        half = out3[14 + core + x // 2]
        for c in range(2):
            r2[x, c, pl.ds(0, 8, stride=2), :] = half
            r2[x, c, pl.ds(1, 8, stride=2), :] = half
    for x in range(1, 9):
        g = g2_ref[x - 1]
        sa2[x] = g * (row2(x) - (OMEGA / g) * r2[x] + coarse_neighbours(r2, x))
    for x in range(2, 8):
        sb = THIRD * sa2[x] + g2_ref[x - 1] * coarse_neighbours(sa2, x)
        out2[x - 2] = 0.5 * (src2[x - 2] + r2[x] + sa2[x] + sb)

    for x in range(12):
        for c in range(4):
            half = out2[x // 2, c // 2]
            r1[x, c, pl.ds(0, 16, stride=2), :] = half
            r1[x, c, pl.ds(1, 16, stride=2), :] = half

    def middle1(x, carry):
        g = g1_ref[x + 2]
        sa1[x] = g * (f1_ref[x - 1] - (OMEGA / g) * r1[x] + coarse_neighbours(r1, x))
        return carry

    lax.fori_loop(1, 11, middle1, 0, unroll=8)

    def last1(x, carry):
        sb = THIRD * sa1[x] + g1_ref[x + 2] * coarse_neighbours(sa1, x)
        row = 0.5 * (src1_ref[x - 2] + r1[x] + sa1[x] + sb)
        for c in range(4):
            out1[x - 2, pl.ds(32 * c, 32), :] = row[c]
        return carry

    lax.fori_loop(2, 10, last1, 0, unroll=8)

    def spread0(x, carry):
        for y in range(8):
            row = out1[x, pl.ds(14 + y, 4, stride=32), :]
            for p in range(2):
                for q in range(2):
                    for c in range(2):
                        r0[2 * x + p, 2 * y + q, pl.ds(c, 4, stride=2), :] = row
        return carry

    lax.fori_loop(0, 8, spread0, 0, unroll=8)
    f0[2:10, 2:10] = f0_ref[...]
    f0[2:10, 0:2] = fylo_ref[...]
    f0[2:10, 10:12] = fyhi_ref[...]
    f0[0:2] = fxlo_ref[...]
    f0[10:12] = fxhi_ref[...]

    def residual0(x, carry):
        g = g0_ref[x]
        f = f0[x] - (OMEGA / g) * r0[x + 2, 2:14] + fine_neighbours(r0, x + 2, 2, 14)
        f0[x] = f
        s3[x] = g * f
        return carry

    lax.fori_loop(0, 12, residual0, 0, unroll=8)

    def first0(x, carry):
        s4[x, 1:11] = THIRD * s3[x, 1:11] + g0_ref[x, 1:11] * fine_neighbours(s3, x, 1, 11)
        return carry

    lax.fori_loop(1, 11, first0, 0, unroll=8)

    def second0(x, carry):
        f4 = THIRD * f0[x, 2:10] + fine_neighbours(s3, x, 2, 10)
        f5 = THIRD * f4 + fine_neighbours(s4, x, 2, 10)
        source = src0_ref[x - 2] + r0[x + 2, 4:12] + s3[x, 2:10] + s4[x, 2:10]
        placed[pl.ds(64 * (x - 2), 64), :] = f5.reshape(64, 128)
        placed[pl.ds(64 * (x - 2) + 512, 64), :] = source.reshape(64, 128)
        return carry

    lax.fori_loop(2, 10, second0, 0, unroll=8)
    for c in range(8):
        turned[pl.ds(c, 128, stride=8), :] = placed[pl.ds(c, 128, stride=8), :].T
    result = turned[...].T
    guess_ref[...] = result[0:64].reshape(8, 8, 1024)
    source_ref[...] = result[64:128].reshape(8, 8, 1024)


def up(index, *arrays):
    scratch = [
        (32, 2, 8, 128), (32, 8, 128), (6, 2, 16, 128), (6, 2, 16, 128),
        (10, 2, 16, 128), (10, 2, 16, 128), (6, 2, 16, 128),
        (12, 4, 32, 128), (12, 4, 32, 128), (8, 128, 128),
        (16, 16, 8, 128), (12, 12, 8, 128), (12, 12, 8, 128), (12, 12, 8, 128),
        (1024, 128), (1024, 128),
    ]
    return pl.pallas_call(
        up_kernel,
        out_shape=(shape(8, 8, 1024), shape(8, 8, 1024)),
        in_specs=[smem()] + [vmem()] * len(arrays),
        scratch_shapes=[pltpu.VMEM(dims, F32) for dims in scratch],
        compiler_params=params(),
    )(index, *arrays)


def shifted(v, axis, count, step):
    return lax.ppermute(v, axis, [(i, (i + step) % count) for i in range(count)])


def swap_core(v):
    return lax.ppermute(v, "gx", [(i, i ^ 1) for i in range(GX)])


def swap_outer(v):
    return lax.ppermute(v, "gx", [(i, (i + 1 if i % 2 else i - 1) % GX) for i in range(GX)])


def skip_chip(v):
    return lax.ppermute(v, "gx", [(i, (i - 2 if i % 2 else i + 2) % GX) for i in range(GX)])


def gather_y(v):
    return lax.all_to_all(jnp.broadcast_to(v[None], (GY,) + v.shape), "gy", 0, 0)


def together(*arrays):
    return lax.optimization_barrier(arrays)


def level1_rows(core, v):
    pair = swap_core(v)
    outer = swap_outer(v)
    skip = skip_chip(jnp.where(core == 0, v[:, 2:4], v[:, 0:2]))
    pair, outer, skip = together(pair, outer, skip)
    far = swap_core(jnp.where(core == 0, outer[:, 2:4], outer[:, 0:2]))
    return v, pair, outer, skip, far


def per_device(cotangent, diagonal):
    core = lax.axis_index("gx") % 2
    index = jnp.stack([lax.axis_index("gx"), lax.axis_index("gy")]).astype(jnp.int32)
    f, sg, ylo, yhi, c1 = prepare(cotangent, diagonal)

    ylo, yhi = shifted(yhi, "gy", GY, 1), shifted(ylo, "gy", GY, -1)
    xlo = jnp.concatenate([ylo[:, 0:2], sg[:, 0:2], yhi[:, 0:2]], axis=2)
    xhi = jnp.concatenate([ylo[:, 6:8], sg[:, 6:8], yhi[:, 6:8]], axis=2)
    xlo, xhi = shifted(xhi, "gx", GX, 1), shifted(xlo, "gx", GX, -1)

    g1, g2, c3 = coefficients(index, *level1_rows(core, gather_y(c1)))

    f2, src0, g0, fylo, fyhi, rhs1 = fine_down(f, sg, ylo, yhi, xlo, xhi)
    fylo, fyhi = shifted(fyhi, "gy", GY, 1), shifted(fylo, "gy", GY, -1)
    fxlo = jnp.concatenate([fylo[0:2], f2[0:2], fyhi[0:2]], axis=1)
    fxhi = jnp.concatenate([fylo[6:8], f2[6:8], fyhi[6:8]], axis=1)
    fxlo, fxhi = shifted(fxhi, "gx", GX, 1), shifted(fxlo, "gx", GX, -1)

    f1, src1, fs2, part2, both3 = middle_down(index, level1_rows(core, gather_y(rhs1)), g1, g2, c3)
    pair2, outer2, skip2 = swap_core(fs2), swap_outer(fs2), skip_chip(part2)
    far2 = swap_core(jnp.where(core == 0, outer2[0, 1], outer2[0, 0]))

    groups = [[c + 2 * k for k in range(16)] for c in range(2)]
    mine3 = lax.all_to_all(jnp.broadcast_to(both3[None], (16,) + both3.shape), "gx", 0, 0, axis_index_groups=groups)
    other3 = swap_core(mine3)

    return up(
        index, mine3, other3, fs2, pair2, outer2, skip2, far2, g2, g1, f1, src1, g0, f2, src0, fylo, fyhi, fxlo, fxhi
    )


def solution(mesh):
    spec = P("gx", "gy", None)
    return jax.shard_map(per_device, mesh=mesh, in_specs=(spec, spec), out_specs=(spec, spec), check_vma=False)
```
